128 devices in a mesh: space: 32 (over y, x, core), tm: 4 (over z).
Axes of the slice: x: 4, y: 4, z: 4, core: 2. Of those that a mesh axis runs over, the one named last changes fastest.
Arguments:
- field: bfloat16 [192, 1440, 1024], P('space', None, 'tm'), may hold values from -72 to 72
- sketch: bfloat16 [192, 1440, 512], P('space'), may hold values from -0.01171875 to 0.01171875
Outputs:
- basis: float32 [1024, 512], P(('tm', 'space'))
- r_factor: float32 [512, 512], replicated
The draws below stay inside these ranges and needn't reach their ends.
All inputs are finite; a program needn't handle non-finite values.
Results may differ from the reference program's by a relative error of at most 0.02.
Values may be sent and summed in bfloat16 or wider, within the bound.
A program may use at most 256 MiB of HBM per device.

```python
import math
import jax
import jax.numpy as jnp
from jax import lax

LON = 1440
K = 512
HALO = 120
H_DEV = 256
LAT_DEV = 6
NLAT = 192
HOURS = 1024
N_SPACE = 32
N_TM = 4


def draw_field(key, part):
    key = jax.random.fold_in(key, 11)
    noise = jax.random.normal(key, (NLAT, LON, HOURS), jnp.float32)
    noise = jnp.clip(noise, -6.0, 6.0)
    rise = 1.75
    position = jnp.arange(HOURS, dtype=jnp.float32) / (HOURS - 1.0)
    amplitude = 4.0 * jnp.exp(jnp.log(rise) * position)
    return (noise * amplitude[None, None, :]).astype(jnp.bfloat16)


def level_of(key, dims, split, low, high):
    loudness, own = 1.0, jax.random.fold_in(key, 6)
    for dim, shards_of in split:
        heights = jnp.exp(jax.random.uniform(jax.random.fold_in(own, dim), (shards_of,), jnp.float32, low / len(split), high / len(split)))
        loudness = loudness * jnp.repeat(heights, dims[dim] // shards_of).reshape([-1 if axis == dim else 1 for axis in range(len(dims))])
    return loudness


def gaussian(rng, dims, scale, reach, shards=(), held_as=jnp.bfloat16):
    values = scale * jax.random.normal(rng, dims, jnp.float32)
    if shards:
        values = values * level_of(rng, dims, shards, -0.22, 0.18)
    return jnp.clip(values, -reach, reach).astype(held_as)


def setup_inputs(seed: int = 0) -> dict:
    seeds = jax.random.split(jax.random.key(seed), 3)
    return {
        "field": draw_field(jax.random.fold_in(seeds[2], 71), 0),
        "sketch": gaussian(seeds[1], (NLAT, LON, K), (NLAT * LON) ** -0.5, 0.01171875, ((0, 32),)),
    }


low_cutoff = 1.0 / 240.0
high_cutoff = 0.4
smooth_taps = (1.0 / 16.0, 4.0 / 16.0, 6.0 / 16.0, 4.0 / 16.0, 1.0 / 16.0)

def band_matrix(span):
    rows_idx = jnp.arange(span + 2 * HALO, dtype=jnp.float32)
    cols_idx = jnp.arange(span, dtype=jnp.float32)
    offset = rows_idx[:, None] - cols_idx[None, :] - HALO
    value = 2.0 * high_cutoff * jnp.sinc(2.0 * high_cutoff * offset) - 2.0 * low_cutoff * jnp.sinc(2.0 * low_cutoff * offset)
    value = value * jnp.sinc(offset / (HALO + 1.0))
    inside = jnp.abs(offset) <= HALO
    return jnp.where(inside, value, jnp.zeros_like(value)).astype(jnp.bfloat16)

def smooth_rows(padded):
    count = padded.shape[0] - 4
    across = smooth_taps[0] * padded[0:count].astype(jnp.float32)
    for shift in range(1, 5):
        across = across + smooth_taps[shift] * padded[shift:shift + count].astype(jnp.float32)
    total = smooth_taps[2] * across
    for shift in (0, 1, 3, 4):
        total = total + smooth_taps[shift] * jnp.roll(across, 2 - shift, axis=1)
    return total.astype(jnp.bfloat16)

def reference(field, sketch):
    padded = jnp.pad(field, ((2, 2), (0, 0), (0, 0)))
    band = band_matrix(H_DEV)

    def one_block(carry, index):
        start = (index * LAT_DEV).astype(jnp.int32)
        rows = lax.dynamic_slice_in_dim(padded, start, LAT_DEV + 4, 0)
        rows = jnp.pad(rows, ((0, 0), (0, 0), (HALO, HALO)))
        smooth = smooth_rows(rows)
        flat = smooth.reshape(-1, HOURS + 2 * HALO)
        pieces = []
        for block in range(N_TM):
            segment = flat[:, block * H_DEV:block * H_DEV + H_DEV + 2 * HALO]
            pieces.append(jnp.dot(segment.astype(jnp.float32), band.astype(jnp.float32), preferred_element_type=jnp.float32).astype(jnp.bfloat16))
        filtered = jnp.concatenate(pieces, axis=1)
        wide = filtered.astype(jnp.float32)
        energy = lax.optimization_barrier(jnp.sum(wide * wide, axis=1))
        inverse = lax.rsqrt(energy / HOURS + 1e-06)
        standard = (wide * inverse[:, None]).astype(jnp.bfloat16)
        omega = lax.dynamic_slice_in_dim(sketch, start, LAT_DEV, 0).reshape(-1, K)
        term = lax.dot_general(standard.astype(jnp.float32), omega.astype(jnp.float32), (((0,), (0,)), ((), ())), preferred_element_type=jnp.float32)
        return (carry + term, None)
    sketched, _ = lax.scan(one_block, jnp.zeros((HOURS, K), jnp.float32), jnp.arange(N_SPACE, dtype=jnp.int32))
    gram = jnp.dot(sketched.T, sketched, precision=lax.Precision.HIGHEST)
    lower = jnp.linalg.cholesky(gram)
    scale = math.sqrt(HOURS)
    solved = jax.scipy.linalg.solve_triangular(lower, sketched.T, lower=True)
    return (solved.T * scale, lower.T / scale)
```

```python
import functools
import math

import jax
import jax.numpy as jnp
from jax import lax
from jax.experimental import pallas as pl
from jax.experimental.pallas import tpu as pltpu
from jax.sharding import PartitionSpec as P

HALO = 120
F32 = jnp.float32
HI = lax.Precision.HIGHEST
MESH = pl.DeviceIdType.MESH


low_cutoff = 1.0 / 240.0
high_cutoff = 0.4
smooth_taps = (1.0 / 16.0, 4.0 / 16.0, 6.0 / 16.0, 4.0 / 16.0, 1.0 / 16.0)


def padded_2(x, sides, width):
    for axis, dim in sides:
        devices, length = (lax.axis_size(axis), x.shape[dim])
        up = [(i, (i + 1) % devices) for i in range(devices - 1)]
        down = [(j, i) for i, j in up]
        last = lax.slice_in_dim(x, length - width, length, axis=dim)
        leading = lax.slice_in_dim(x, 0, width, axis=dim)
        before = lax.ppermute(last, axis, up)
        after = lax.ppermute(leading, axis, down)
        x = jnp.concatenate([before, x, after], axis=dim)
    return x


def band_matrix(span):
    rows_idx = jnp.arange(span + 2 * HALO, dtype=jnp.float32)
    cols_idx = jnp.arange(span, dtype=jnp.float32)
    offset = rows_idx[:, None] - cols_idx[None, :] - HALO
    value = 2.0 * high_cutoff * jnp.sinc(2.0 * high_cutoff * offset) - 2.0 * low_cutoff * jnp.sinc(
        2.0 * low_cutoff * offset
    )
    value = value * jnp.sinc(offset / (HALO + 1.0))
    inside = jnp.abs(offset) <= HALO
    return jnp.where(inside, value, jnp.zeros_like(value)).astype(jnp.bfloat16)


def smooth_rows(padded):
    count = padded.shape[0] - 4
    across = smooth_taps[0] * padded[0:count].astype(jnp.float32)
    for shift in range(1, 5):
        across = across + smooth_taps[shift] * padded[shift : shift + count].astype(jnp.float32)
    total = smooth_taps[2] * across
    for shift in (0, 1, 3, 4):
        total = total + smooth_taps[shift] * jnp.roll(across, 2 - shift, axis=1)
    return total.astype(jnp.bfloat16)


def gather_kernel(part_ref, all_ref, own_ref, arrived, send_sem, recv_sem, out_sem, in_sem, pair_sem):
    spaces, blocks = lax.axis_size("space"), lax.axis_size("tm")
    chips = spaces // 2
    flat = chips * blocks
    s, t = lax.axis_index("space"), lax.axis_index("tm")
    core, chip = lax.rem(s, 2), s // 2
    sibling = 2 * chip + 1 - core
    mine = chip * blocks + t
    rows = own_ref.shape[0]

    def across(q):
        return lax.rem(s + q, spaces), t

    def around(e):
        to = lax.rem(mine + e, flat)
        return 2 * (to // blocks) + core, lax.rem(to, blocks)

    barrier = pltpu.get_barrier_semaphore()

    @pl.loop(1, spaces)
    def _(q):
        pl.semaphore_signal(barrier, inc=1, device_id=across(q), device_id_type=MESH)

    @pl.loop(1, flat)
    def _(e):
        pl.semaphore_signal(barrier, inc=1, device_id=around(e), device_id_type=MESH)

    pl.semaphore_wait(barrier, spaces + flat - 2)

    @pl.loop(1, spaces)
    def _(q):
        to, _ = across(q)
        pltpu.make_async_remote_copy(
            src_ref=part_ref.at[pl.ds(pl.multiple_of(to * rows, rows), rows)],
            dst_ref=arrived.at[q - 1],
            send_sem=send_sem,
            recv_sem=recv_sem,
            device_id=across(q),
            device_id_type=MESH,
        ).start()

    landed = pltpu.make_async_copy(arrived, arrived, recv_sem)
    landed.wait()
    total = part_ref[pl.ds(pl.multiple_of(s * rows, rows), rows), :]
    for q in range(spaces - 1):
        total = total + arrived[q]
    own_ref[...] = total
    all_ref[core, mine] = total

    @pl.loop(1, flat)
    def _(e):
        pltpu.make_async_remote_copy(
            src_ref=own_ref,
            dst_ref=all_ref.at[core, mine],
            send_sem=out_sem,
            recv_sem=in_sem,
            device_id=around(e),
            device_id_type=MESH,
        ).start()

    others = all_ref.at[core, pl.ds(0, flat - 1)]
    pltpu.make_async_copy(others, others, in_sem).wait()
    pair = pltpu.make_async_remote_copy(
        src_ref=all_ref.at[core],
        dst_ref=all_ref.at[core],
        send_sem=pair_sem.at[0],
        recv_sem=pair_sem.at[1],
        device_id=(sibling, t),
        device_id_type=MESH,
    )
    pair.start()
    pltpu.make_async_copy(arrived, arrived, send_sem).wait()
    pltpu.make_async_copy(others, others, out_sem).wait()
    pair.wait()


def gather(part, spaces, blocks):
    hours, n = part.shape
    rows = hours // spaces
    flat = spaces // 2 * blocks
    vmem = pl.BlockSpec(memory_space=pltpu.VMEM)
    return pl.pallas_call(
        gather_kernel,
        out_shape=(
            jax.ShapeDtypeStruct((2, flat, rows, n), F32),
            jax.ShapeDtypeStruct((rows, n), F32),
        ),
        in_specs=[vmem],
        out_specs=(vmem, vmem),
        scratch_shapes=[
            pltpu.VMEM((spaces - 1, rows, n), F32),
            pltpu.SemaphoreType.DMA,
            pltpu.SemaphoreType.DMA,
            pltpu.SemaphoreType.DMA,
            pltpu.SemaphoreType.DMA,
            pltpu.SemaphoreType.DMA((2,)),
        ],
        compiler_params=pltpu.CompilerParams(
            collective_id=0, has_side_effects=True, vmem_limit_bytes=32 * 2**20
        ),
        name="gather",
    )(part)


def factor_block(m_ref):
    lane8 = lax.broadcasted_iota(jnp.int32, (8, 1), 0)
    for q in range(16):
        top = 8 * q
        p = m_ref[top:top + 8, :]
        cols = [jnp.broadcast_to(m_ref[top:128, top + k:top + k + 1], (128 - top, 128)) for k in range(8)]
        scaled = []
        for k in range(8):
            c = cols[k]
            d = c[k:k + 1, :]
            r = 1.0 / d
            for m in range(k + 1, 8):
                cols[m] = cols[m] - c * (cols[m][k:k + 1, :] * r)
            row = p[k:k + 1, :]
            t = row * jnp.concatenate([r, r], axis=1)
            below = jnp.where(lane8 > k, c[0:8, :], 0.0)
            p = p - jnp.concatenate([below, below], axis=1) * t
            scaled.append(t)
            s = lax.rsqrt(d)
            m_ref[top + k:top + k + 1, :] = row * jnp.concatenate([s, s], axis=1)
        if q < 15:
            left = m_ref[top + 8:128, 0:128]
            right = m_ref[top + 8:128, 128:256]
            for k in range(8):
                c = cols[k][8:, :]
                left = left - c * scaled[k][:, 0:128]
                right = right - c * scaled[k][:, 128:256]
            m_ref[top + 8:128, 0:128] = left
            m_ref[top + 8:128, 128:256] = right

def factor_kernel(root, y_ref, own_ref, basis_ref, r_ref, a_ref, m_ref, rest_ref):
    n = y_ref.shape[1]
    blocks = n // 128
    a_ref[...] = lax.dot_general(y_ref[...], y_ref[...], (((0,), (0,)), ((), ())), precision=HI, preferred_element_type=F32)
    rest_ref[...] = own_ref[...]
    row = lax.broadcasted_iota(jnp.int32, (128, 128), 0)
    col = lax.broadcasted_iota(jnp.int32, (128, 128), 1)

    @pl.loop(0, blocks)
    def _(b):
        here = pl.ds(pl.multiple_of(b * 128, 128), 128)
        m_ref[:, 0:128] = a_ref[here, here]
        m_ref[:, 128:256] = (row == col).astype(F32)
        factor_block(m_ref)
        inv = m_ref[:, 128:256]
        x = lax.dot_general(rest_ref[:, here], inv, (((1,), (1,)), ((), ())), precision=HI, preferred_element_type=F32)
        basis_ref[:, here] = x * root
        panel = jnp.dot(inv, a_ref[here, :], precision=HI, preferred_element_type=F32)
        wide = lax.broadcasted_iota(jnp.int32, (128, n), 1) >= (b + 1) * 128
        panel = jnp.where(wide, panel, 0.0)
        r_ref[here, :] = panel * (1.0 / root)
        r_ref[here, here] = jnp.where(row <= col, m_ref[:, 0:128], 0.0) * (1.0 / root)
        rest_ref[...] -= jnp.dot(x, panel, precision=HI, preferred_element_type=F32)
        a_ref[...] -= lax.dot_general(panel, panel, (((0,), (0,)), ((), ())), precision=HI, preferred_element_type=F32)

def factor(y, own, hours):
    n = y.shape[1]
    return pl.pallas_call(
        functools.partial(factor_kernel, math.sqrt(hours)),
        out_shape=(jax.ShapeDtypeStruct((own.shape[0], n), F32), jax.ShapeDtypeStruct((n, n), F32)),
        in_specs=[pl.BlockSpec(memory_space=pltpu.VMEM)] * 2,
        out_specs=(pl.BlockSpec(memory_space=pltpu.VMEM), pl.BlockSpec(memory_space=pltpu.VMEM)),
        scratch_shapes=[pltpu.VMEM((n, n), F32), pltpu.VMEM((128, 256), F32), pltpu.VMEM((own.shape[0], n), F32)],
        compiler_params=pltpu.CompilerParams(vmem_limit_bytes=32 * 2**20),
        name="factor",
    )(y, own)


def body(field, sketch):
    block_hours = field.shape[2]
    widened = padded_2(field, (("tm", 2),), HALO)
    taller = padded_2(widened, (("space", 0),), 2)
    smooth = smooth_rows(taller)
    flat = smooth.reshape(-1, block_hours + 2 * HALO)
    band = band_matrix(block_hours)
    filtered = jnp.dot(flat, band, preferred_element_type=jnp.float32).astype(jnp.bfloat16)
    wide = filtered.astype(jnp.float32)
    energy = lax.psum(jnp.sum(wide * wide, axis=1), "tm")
    all_hours = block_hours * lax.axis_size("tm")
    inverse = lax.rsqrt(energy / all_hours + 1e-06)
    standard = (wide * inverse[:, None]).astype(jnp.bfloat16)
    omega = sketch.reshape(-1, sketch.shape[2])
    columns = lax.slice_in_dim(
        standard, 0, lax.axis_size("space") * (block_hours // lax.axis_size("space")), axis=1
    )
    part = lax.dot_general(columns, omega, (((0,), (0,)), ((), ())), preferred_element_type=jnp.float32)
    everyone, own = gather(part, lax.axis_size("space"), lax.axis_size("tm"))
    return factor(everyone.reshape(all_hours, -1), own, all_hours)


def solution(mesh):
    placed = (P("space", None, "tm"), P("space", None, None))
    return jax.shard_map(
        body, mesh=mesh, in_specs=placed, out_specs=(P(("tm", "space"), None), P()), check_vma=False
    )
```

```python
import functools
import math

import jax
import jax.numpy as jnp
import numpy as np
from jax import lax
from jax.experimental import pallas as pl
from jax.experimental.pallas import tpu as pltpu
from jax.sharding import PartitionSpec as P

HALO = 120
F32 = jnp.float32
HI = lax.Precision.HIGHEST
MESH = pl.DeviceIdType.MESH


low_cutoff = 1.0 / 240.0
high_cutoff = 0.4
smooth_taps = (1.0 / 16.0, 4.0 / 16.0, 6.0 / 16.0, 4.0 / 16.0, 1.0 / 16.0)


def band_weights(span):
    m = np.arange(span + 256, dtype=np.float64)[None, :] - 128.0 - np.arange(span, dtype=np.float64)[:, None]
    value = 2.0 * high_cutoff * np.sinc(2.0 * high_cutoff * m) - 2.0 * low_cutoff * np.sinc(2.0 * low_cutoff * m)
    value = value * np.sinc(m / (HALO + 1.0))
    return np.where(np.abs(m) <= HALO, value, 0.0).astype(np.float32).astype(jnp.bfloat16)


def ring_weights(piece):
    offset = np.arange(piece + 32)[None, :] - 16 - np.arange(piece)[:, None]
    value = np.zeros(offset.shape, np.float32)
    for shift in range(-2, 3):
        value = np.where(offset == shift, smooth_taps[shift + 2], value)
    return value.astype(jnp.bfloat16)


def front_kernel(
    hours,
    field_ref,
    sketch_ref,
    band_ref,
    ring_ref,
    part_ref,
    x,
    series,
    omega,
    filtered,
    energy,
    heard,
    load_sem,
    omega_sem,
    row_sem,
    rim_sem,
    energy_out,
    energy_in,
):
    spaces, blocks = lax.axis_size("space"), lax.axis_size("tm")
    s, t = lax.axis_index("space"), lax.axis_index("tm")
    rows, lon, span = field_ref.shape
    piece = ring_ref.shape[0]
    last = rows + 2

    own = pltpu.make_async_copy(field_ref, x.at[2:last, 16 : lon + 16], load_sem.at[0])
    left = pltpu.make_async_copy(field_ref.at[:, lon - 16 : lon], x.at[2:last, 0:16], load_sem.at[1])
    right = pltpu.make_async_copy(field_ref.at[:, 0:16], x.at[2:last, lon + 16 : lon + 32], load_sem.at[2])
    own.start()
    left.start()
    right.start()
    load_omega = pltpu.make_async_copy(sketch_ref, omega, omega_sem)

    barrier = pltpu.get_barrier_semaphore()
    for q in range(1, blocks):
        pl.semaphore_signal(barrier, inc=1, device_id=(s, lax.rem(t + q, blocks)), device_id_type=MESH)

    @pl.when(s > 0)
    def _():
        pl.semaphore_signal(barrier, inc=1, device_id=(s - 1, t), device_id_type=MESH)

    @pl.when(s < spaces - 1)
    def _():
        pl.semaphore_signal(barrier, inc=1, device_id=(s + 1, t), device_id_type=MESH)

    pl.semaphore_wait(barrier, blocks - 1 + jnp.where(s > 0, 1, 0) + jnp.where(s < spaces - 1, 1, 0))

    up = pltpu.make_async_remote_copy(
        src_ref=field_ref.at[rows - 2 : rows],
        dst_ref=x.at[0:2, 16 : lon + 16],
        send_sem=row_sem.at[0],
        recv_sem=row_sem.at[1],
        device_id=(s + 1, t),
        device_id_type=MESH,
    )
    down = pltpu.make_async_remote_copy(
        src_ref=field_ref.at[0:2],
        dst_ref=x.at[last : last + 2, 16 : lon + 16],
        send_sem=row_sem.at[2],
        recv_sem=row_sem.at[3],
        device_id=(s - 1, t),
        device_id_type=MESH,
    )

    @pl.when(s < spaces - 1)
    def _():
        up.start()

    @pl.when(s > 0)
    def _():
        down.start()

    own.wait()
    left.wait()
    right.wait()
    load_omega.start()

    def smooth(first):
        @pl.loop(0, lon // piece)
        def _(c):
            at = pl.multiple_of(c * piece, 16)
            across = [
                jnp.dot(ring_ref[...], x[first + r, pl.ds(at, piece + 32), :], preferred_element_type=F32)
                for r in range(6)
            ]
            for r in range(2):
                total = smooth_taps[2] * across[r + 2] + smooth_taps[1] * (across[r + 1] + across[r + 3])
                total = total + smooth_taps[0] * (across[r] + across[r + 4])
                series[first + r, pl.ds(at, piece), 128 : 128 + span] = total.astype(jnp.bfloat16)

    def rims(i):
        before = pltpu.make_async_remote_copy(
            src_ref=series.at[i, :, span : span + 128],
            dst_ref=series.at[i, :, 0:128],
            send_sem=rim_sem.at[0, i],
            recv_sem=rim_sem.at[1, i],
            device_id=(s, t + 1),
            device_id_type=MESH,
        )
        after = pltpu.make_async_remote_copy(
            src_ref=series.at[i, :, 128:256],
            dst_ref=series.at[i, :, span + 128 : span + 256],
            send_sem=rim_sem.at[2, i],
            recv_sem=rim_sem.at[3, i],
            device_id=(s, t - 1),
            device_id_type=MESH,
        )
        return before, after

    def send_rims(first):
        for r in range(2):
            before, after = rims(first + r)

            @pl.when(t < blocks - 1)
            def _():
                before.start()

            @pl.when(t > 0)
            def _():
                after.start()

    smooth(2)
    send_rims(2)

    @pl.when(t == 0)
    def _():
        series[:, :, 0:128] = jnp.zeros((rows, lon, 128), jnp.bfloat16)

    @pl.when(t == blocks - 1)
    def _():
        series[:, :, span + 128 : span + 256] = jnp.zeros((rows, lon, 128), jnp.bfloat16)

    @pl.when(s < spaces - 1)
    def _():
        down.wait_recv()

    @pl.when(s == spaces - 1)
    def _():
        x[last : last + 2, 16 : lon + 16] = jnp.zeros((2, lon, span), jnp.bfloat16)

    x[last : last + 2, 0:16] = x[last : last + 2, lon : lon + 16]
    x[last : last + 2, lon + 16 : lon + 32] = x[last : last + 2, 16:32]
    smooth(4)
    send_rims(4)

    @pl.when(s > 0)
    def _():
        up.wait_recv()

    @pl.when(s == 0)
    def _():
        x[0:2, 16 : lon + 16] = jnp.zeros((2, lon, span), jnp.bfloat16)

    x[0:2, 0:16] = x[0:2, lon : lon + 16]
    x[0:2, lon + 16 : lon + 32] = x[0:2, 16:32]
    smooth(0)
    send_rims(0)

    def energy_copy(i, q):
        return pltpu.make_async_remote_copy(
            src_ref=energy.at[i],
            dst_ref=heard.at[i, q - 1],
            send_sem=energy_out.at[i],
            recv_sem=energy_in.at[i],
            device_id=(s, lax.rem(t + q, blocks)),
            device_id_type=MESH,
        )

    def filter_row(i):
        before, after = rims(i)

        @pl.when(t > 0)
        def _():
            before.wait_recv()

        @pl.when(t < blocks - 1)
        def _():
            after.wait_recv()

        value = lax.dot_general(
            band_ref[...], series[i], (((1,), (1,)), ((), ())), preferred_element_type=F32
        ).astype(jnp.bfloat16)
        filtered[i] = value
        wide = value.astype(F32)
        energy[i] = jnp.sum(wide * wide, axis=0, keepdims=True)
        for q in range(1, blocks):
            energy_copy(i, q).start()

    def sketch_row(i):
        pltpu.make_async_copy(heard.at[i], heard.at[i], energy_in.at[i]).wait()
        total = energy[i]
        for q in range(blocks - 1):
            total = total + heard[i, q]
        inverse = lax.rsqrt(total / hours + 1e-06)
        standard = (filtered[i].astype(F32) * inverse).astype(jnp.bfloat16)
        part_ref[...] += jnp.dot(standard, omega[i], preferred_element_type=F32)

    part_ref[...] = jnp.zeros(part_ref.shape, F32)
    load_omega.wait()

    @pl.loop(0, rows + 1)
    def _(n):
        @pl.when(n < rows)
        def _():
            filter_row(lax.rem(n + 2, rows))

        @pl.when(n > 0)
        def _():
            sketch_row(lax.rem(n + 1, rows))

    @pl.when(s < spaces - 1)
    def _():
        up.wait_send()

    @pl.when(s > 0)
    def _():
        down.wait_send()

    for i in range(rows):
        before, after = rims(i)

        @pl.when(t < blocks - 1)
        def _():
            before.wait_send()

        @pl.when(t > 0)
        def _():
            after.wait_send()

        pltpu.make_async_copy(heard.at[i], heard.at[i], energy_out.at[i]).wait()


def front(field, sketch, spaces, blocks):
    rows, lon, span = field.shape
    n = sketch.shape[2]
    piece = 144
    vmem = pl.BlockSpec(memory_space=pltpu.VMEM)
    hbm = pl.BlockSpec(memory_space=pl.ANY)
    return pl.pallas_call(
        functools.partial(front_kernel, span * blocks),
        out_shape=jax.ShapeDtypeStruct((span, n), F32),
        in_specs=[hbm, hbm, vmem, vmem],
        out_specs=vmem,
        scratch_shapes=[
            pltpu.VMEM((rows + 4, lon + 32, span), jnp.bfloat16),
            pltpu.VMEM((rows, lon, span + 256), jnp.bfloat16),
            pltpu.VMEM((rows, lon, n), jnp.bfloat16),
            pltpu.VMEM((rows, span, lon), jnp.bfloat16),
            pltpu.VMEM((rows, 1, lon), F32),
            pltpu.VMEM((rows, blocks - 1, 1, lon), F32),
            pltpu.SemaphoreType.DMA((3,)),
            pltpu.SemaphoreType.DMA,
            pltpu.SemaphoreType.DMA((4,)),
            pltpu.SemaphoreType.DMA((4, rows)),
            pltpu.SemaphoreType.DMA((rows,)),
            pltpu.SemaphoreType.DMA((rows,)),
        ],
        compiler_params=pltpu.CompilerParams(
            collective_id=1, has_side_effects=True, vmem_limit_bytes=56 * 2**20
        ),
        name="front",
    )(field, sketch, jnp.asarray(band_weights(span)), jnp.asarray(ring_weights(piece)))


def gather_kernel(part_ref, all_ref, own_ref, arrived, send_sem, recv_sem, out_sem, in_sem, pair_sem):
    spaces, blocks = lax.axis_size("space"), lax.axis_size("tm")
    chips = spaces // 2
    flat = chips * blocks
    s, t = lax.axis_index("space"), lax.axis_index("tm")
    core, chip = lax.rem(s, 2), s // 2
    sibling = 2 * chip + 1 - core
    mine = chip * blocks + t
    rows = own_ref.shape[0]

    def across(q):
        return lax.rem(s + q, spaces), t

    def around(e):
        to = lax.rem(mine + e, flat)
        return 2 * (to // blocks) + core, lax.rem(to, blocks)

    barrier = pltpu.get_barrier_semaphore()

    @pl.loop(1, spaces)
    def _(q):
        pl.semaphore_signal(barrier, inc=1, device_id=across(q), device_id_type=MESH)

    @pl.loop(1, flat)
    def _(e):
        pl.semaphore_signal(barrier, inc=1, device_id=around(e), device_id_type=MESH)

    pl.semaphore_wait(barrier, spaces + flat - 2)

    @pl.loop(1, spaces)
    def _(q):
        to, _ = across(q)
        pltpu.make_async_remote_copy(
            src_ref=part_ref.at[pl.ds(pl.multiple_of(to * rows, rows), rows)],
            dst_ref=arrived.at[q - 1],
            send_sem=send_sem,
            recv_sem=recv_sem,
            device_id=across(q),
            device_id_type=MESH,
        ).start()

    landed = pltpu.make_async_copy(arrived, arrived, recv_sem)
    landed.wait()
    total = part_ref[pl.ds(pl.multiple_of(s * rows, rows), rows), :]
    for q in range(spaces - 1):
        total = total + arrived[q]
    own_ref[...] = total
    all_ref[core, mine] = total

    @pl.loop(1, flat)
    def _(e):
        pltpu.make_async_remote_copy(
            src_ref=own_ref,
            dst_ref=all_ref.at[core, mine],
            send_sem=out_sem,
            recv_sem=in_sem,
            device_id=around(e),
            device_id_type=MESH,
        ).start()

    others = all_ref.at[core, pl.ds(0, flat - 1)]
    pltpu.make_async_copy(others, others, in_sem).wait()
    pair = pltpu.make_async_remote_copy(
        src_ref=all_ref.at[core],
        dst_ref=all_ref.at[core],
        send_sem=pair_sem.at[0],
        recv_sem=pair_sem.at[1],
        device_id=(sibling, t),
        device_id_type=MESH,
    )
    pair.start()
    pltpu.make_async_copy(arrived, arrived, send_sem).wait()
    pltpu.make_async_copy(others, others, out_sem).wait()
    pair.wait()


def gather(part, spaces, blocks):
    hours, n = part.shape
    rows = hours // spaces
    flat = spaces // 2 * blocks
    vmem = pl.BlockSpec(memory_space=pltpu.VMEM)
    return pl.pallas_call(
        gather_kernel,
        out_shape=(
            jax.ShapeDtypeStruct((2, flat, rows, n), F32),
            jax.ShapeDtypeStruct((rows, n), F32),
        ),
        in_specs=[vmem],
        out_specs=(vmem, vmem),
        scratch_shapes=[
            pltpu.VMEM((spaces - 1, rows, n), F32),
            pltpu.SemaphoreType.DMA,
            pltpu.SemaphoreType.DMA,
            pltpu.SemaphoreType.DMA,
            pltpu.SemaphoreType.DMA,
            pltpu.SemaphoreType.DMA((2,)),
        ],
        compiler_params=pltpu.CompilerParams(
            collective_id=0, has_side_effects=True, vmem_limit_bytes=32 * 2**20
        ),
        name="gather",
    )(part)


def factor_block(m_ref):
    lane8 = lax.broadcasted_iota(jnp.int32, (8, 1), 0)
    for q in range(16):
        top = 8 * q
        p = m_ref[top:top + 8, :]
        cols = [jnp.broadcast_to(m_ref[top:128, top + k:top + k + 1], (128 - top, 128)) for k in range(8)]
        scaled = []
        for k in range(8):
            c = cols[k]
            d = c[k:k + 1, :]
            r = 1.0 / d
            for m in range(k + 1, 8):
                cols[m] = cols[m] - c * (cols[m][k:k + 1, :] * r)
            row = p[k:k + 1, :]
            t = row * jnp.concatenate([r, r], axis=1)
            below = jnp.where(lane8 > k, c[0:8, :], 0.0)
            p = p - jnp.concatenate([below, below], axis=1) * t
            scaled.append(t)
            s = lax.rsqrt(d)
            m_ref[top + k:top + k + 1, :] = row * jnp.concatenate([s, s], axis=1)
        if q < 15:
            left = m_ref[top + 8:128, 0:128]
            right = m_ref[top + 8:128, 128:256]
            for k in range(8):
                c = cols[k][8:, :]
                left = left - c * scaled[k][:, 0:128]
                right = right - c * scaled[k][:, 128:256]
            m_ref[top + 8:128, 0:128] = left
            m_ref[top + 8:128, 128:256] = right

def factor_kernel(root, y_ref, own_ref, basis_ref, r_ref, a_ref, m_ref, rest_ref):
    n = y_ref.shape[1]
    blocks = n // 128
    a_ref[...] = lax.dot_general(y_ref[...], y_ref[...], (((0,), (0,)), ((), ())), precision=HI, preferred_element_type=F32)
    rest_ref[...] = own_ref[...]
    row = lax.broadcasted_iota(jnp.int32, (128, 128), 0)
    col = lax.broadcasted_iota(jnp.int32, (128, 128), 1)

    @pl.loop(0, blocks)
    def _(b):
        here = pl.ds(pl.multiple_of(b * 128, 128), 128)
        m_ref[:, 0:128] = a_ref[here, here]
        m_ref[:, 128:256] = (row == col).astype(F32)
        factor_block(m_ref)
        inv = m_ref[:, 128:256]
        x = lax.dot_general(rest_ref[:, here], inv, (((1,), (1,)), ((), ())), precision=HI, preferred_element_type=F32)
        basis_ref[:, here] = x * root
        panel = jnp.dot(inv, a_ref[here, :], precision=HI, preferred_element_type=F32)
        wide = lax.broadcasted_iota(jnp.int32, (128, n), 1) >= (b + 1) * 128
        panel = jnp.where(wide, panel, 0.0)
        r_ref[here, :] = panel * (1.0 / root)
        r_ref[here, here] = jnp.where(row <= col, m_ref[:, 0:128], 0.0) * (1.0 / root)
        rest_ref[...] -= jnp.dot(x, panel, precision=HI, preferred_element_type=F32)
        a_ref[...] -= lax.dot_general(panel, panel, (((0,), (0,)), ((), ())), precision=HI, preferred_element_type=F32)

def factor(y, own, hours):
    n = y.shape[1]
    return pl.pallas_call(
        functools.partial(factor_kernel, math.sqrt(hours)),
        out_shape=(jax.ShapeDtypeStruct((own.shape[0], n), F32), jax.ShapeDtypeStruct((n, n), F32)),
        in_specs=[pl.BlockSpec(memory_space=pltpu.VMEM)] * 2,
        out_specs=(pl.BlockSpec(memory_space=pltpu.VMEM), pl.BlockSpec(memory_space=pltpu.VMEM)),
        scratch_shapes=[pltpu.VMEM((n, n), F32), pltpu.VMEM((128, 256), F32), pltpu.VMEM((own.shape[0], n), F32)],
        compiler_params=pltpu.CompilerParams(vmem_limit_bytes=32 * 2**20),
        name="factor",
    )(y, own)


def body(field, sketch):
    spaces, blocks = lax.axis_size("space"), lax.axis_size("tm")
    all_hours = field.shape[2] * blocks
    part = front(field, sketch, spaces, blocks)
    everyone, own = gather(part, spaces, blocks)
    return factor(everyone.reshape(all_hours, -1), own, all_hours)


def solution(mesh):
    placed = (P("space", None, "tm"), P("space", None, None))
    return jax.shard_map(
        body, mesh=mesh, in_specs=placed, out_specs=(P(("tm", "space"), None), P()), check_vma=False
    )
```

```python
import functools
import math

import jax
import jax.numpy as jnp
import numpy as np
from jax import lax
from jax.experimental import pallas as pl
from jax.experimental.pallas import tpu as pltpu
from jax.sharding import PartitionSpec as P

HALO = 120
F32 = jnp.float32
HI = lax.Precision.HIGHEST
MESH = pl.DeviceIdType.MESH


low_cutoff = 1.0 / 240.0
high_cutoff = 0.4
smooth_taps = (1.0 / 16.0, 4.0 / 16.0, 6.0 / 16.0, 4.0 / 16.0, 1.0 / 16.0)


def band_weights(span):
    m = np.arange(span + 256, dtype=np.float64)[None, :] - 128.0 - np.arange(span, dtype=np.float64)[:, None]
    value = 2.0 * high_cutoff * np.sinc(2.0 * high_cutoff * m) - 2.0 * low_cutoff * np.sinc(2.0 * low_cutoff * m)
    value = value * np.sinc(m / (HALO + 1.0))
    return np.where(np.abs(m) <= HALO, value, 0.0).astype(np.float32).astype(jnp.bfloat16)


def ring_weights(piece):
    offset = np.arange(piece + 32)[None, :] - 16 - np.arange(piece)[:, None]
    value = np.zeros(offset.shape, np.float32)
    for shift in range(-2, 3):
        value = np.where(offset == shift, smooth_taps[shift + 2], value)
    return value.astype(jnp.bfloat16)


def front_kernel(
    hours,
    field_ref,
    sketch_ref,
    band_ref,
    ring_ref,
    all_ref,
    own_ref,
    x,
    series,
    omega,
    filtered,
    energy,
    heard,
    load_sem,
    omega_sem,
    row_sem,
    rim_sem,
    energy_out,
    energy_in,
    part,
    offered,
    arrived,
    mine_ref,
    sum_sem,
    gather_sem,
    pair_sem,
):
    spaces, blocks = lax.axis_size("space"), lax.axis_size("tm")
    s, t = lax.axis_index("space"), lax.axis_index("tm")
    rows, lon, span = field_ref.shape
    piece = ring_ref.shape[0]
    last = rows + 2
    core, chip = lax.rem(s, 2), s // 2
    flat = spaces // 2 * blocks
    mine = chip * blocks + t

    def across(q):
        return lax.rem(s + q, spaces), t

    def around(e):
        to = lax.rem(mine + e, flat)
        return 2 * (to // blocks) + core, lax.rem(to, blocks)

    own = pltpu.make_async_copy(field_ref, x.at[2:last, 16 : lon + 16], load_sem.at[0])
    left = pltpu.make_async_copy(field_ref.at[:, lon - 16 : lon], x.at[2:last, 0:16], load_sem.at[1])
    right = pltpu.make_async_copy(field_ref.at[:, 0:16], x.at[2:last, lon + 16 : lon + 32], load_sem.at[2])
    own.start()
    left.start()
    right.start()
    load_omega = pltpu.make_async_copy(sketch_ref, omega, omega_sem)

    barrier = pltpu.get_barrier_semaphore()

    @pl.loop(1, spaces)
    def _(q):
        pl.semaphore_signal(barrier, inc=1, device_id=across(q), device_id_type=MESH)

    @pl.loop(1, flat)
    def _(e):
        pl.semaphore_signal(barrier, inc=1, device_id=around(e), device_id_type=MESH)

    pl.semaphore_wait(barrier, spaces + flat - 2)

    up = pltpu.make_async_remote_copy(
        src_ref=field_ref.at[rows - 2 : rows],
        dst_ref=x.at[0:2, 16 : lon + 16],
        send_sem=row_sem.at[0],
        recv_sem=row_sem.at[1],
        device_id=(s + 1, t),
        device_id_type=MESH,
    )
    down = pltpu.make_async_remote_copy(
        src_ref=field_ref.at[0:2],
        dst_ref=x.at[last : last + 2, 16 : lon + 16],
        send_sem=row_sem.at[2],
        recv_sem=row_sem.at[3],
        device_id=(s - 1, t),
        device_id_type=MESH,
    )

    @pl.when(s < spaces - 1)
    def _():
        up.start()

    @pl.when(s > 0)
    def _():
        down.start()

    own.wait()
    left.wait()
    right.wait()
    load_omega.start()

    def smooth(first):
        @pl.loop(0, lon // piece)
        def _(c):
            at = pl.multiple_of(c * piece, 16)
            across = [
                jnp.dot(ring_ref[...], x[first + r, pl.ds(at, piece + 32), :], preferred_element_type=F32)
                for r in range(6)
            ]
            for r in range(2):
                total = smooth_taps[2] * across[r + 2] + smooth_taps[1] * (across[r + 1] + across[r + 3])
                total = total + smooth_taps[0] * (across[r] + across[r + 4])
                series[first + r, pl.ds(at, piece), 128 : 128 + span] = total.astype(jnp.bfloat16)

    def rims(i):
        before = pltpu.make_async_remote_copy(
            src_ref=series.at[i, :, span : span + 128],
            dst_ref=series.at[i, :, 0:128],
            send_sem=rim_sem.at[0, i],
            recv_sem=rim_sem.at[1, i],
            device_id=(s, t + 1),
            device_id_type=MESH,
        )
        after = pltpu.make_async_remote_copy(
            src_ref=series.at[i, :, 128:256],
            dst_ref=series.at[i, :, span + 128 : span + 256],
            send_sem=rim_sem.at[2, i],
            recv_sem=rim_sem.at[3, i],
            device_id=(s, t - 1),
            device_id_type=MESH,
        )
        return before, after

    def send_rims(first):
        for r in range(2):
            before, after = rims(first + r)

            @pl.when(t < blocks - 1)
            def _():
                before.start()

            @pl.when(t > 0)
            def _():
                after.start()

    smooth(2)
    send_rims(2)

    @pl.when(t == 0)
    def _():
        series[:, :, 0:128] = jnp.zeros((rows, lon, 128), jnp.bfloat16)

    @pl.when(t == blocks - 1)
    def _():
        series[:, :, span + 128 : span + 256] = jnp.zeros((rows, lon, 128), jnp.bfloat16)

    @pl.when(s < spaces - 1)
    def _():
        down.wait_recv()

    @pl.when(s == spaces - 1)
    def _():
        x[last : last + 2, 16 : lon + 16] = jnp.zeros((2, lon, span), jnp.bfloat16)

    x[last : last + 2, 0:16] = x[last : last + 2, lon : lon + 16]
    x[last : last + 2, lon + 16 : lon + 32] = x[last : last + 2, 16:32]
    smooth(4)
    send_rims(4)

    @pl.when(s > 0)
    def _():
        up.wait_recv()

    @pl.when(s == 0)
    def _():
        x[0:2, 16 : lon + 16] = jnp.zeros((2, lon, span), jnp.bfloat16)

    x[0:2, 0:16] = x[0:2, lon : lon + 16]
    x[0:2, lon + 16 : lon + 32] = x[0:2, 16:32]
    smooth(0)
    send_rims(0)

    def energy_copy(i, q):
        return pltpu.make_async_remote_copy(
            src_ref=energy.at[i],
            dst_ref=heard.at[i, q - 1],
            send_sem=energy_out.at[i],
            recv_sem=energy_in.at[i],
            device_id=(s, lax.rem(t + q, blocks)),
            device_id_type=MESH,
        )

    def filter_row(i):
        before, after = rims(i)

        @pl.when(t > 0)
        def _():
            before.wait_recv()

        @pl.when(t < blocks - 1)
        def _():
            after.wait_recv()

        value = lax.dot_general(
            band_ref[...], series[i], (((1,), (1,)), ((), ())), preferred_element_type=F32
        ).astype(jnp.bfloat16)
        filtered[i] = value
        wide = value.astype(F32)
        energy[i] = jnp.sum(wide * wide, axis=0, keepdims=True)
        for q in range(1, blocks):
            energy_copy(i, q).start()

    def sketch_row(i):
        pltpu.make_async_copy(heard.at[i], heard.at[i], energy_in.at[i]).wait()
        total = energy[i]
        for q in range(blocks - 1):
            total = total + heard[i, q]
        inverse = lax.rsqrt(total / hours + 1e-06)
        standard = (filtered[i].astype(F32) * inverse).astype(jnp.bfloat16)
        part[...] += jnp.dot(standard, omega[i], preferred_element_type=F32)

    part[...] = jnp.zeros(part.shape, F32)
    load_omega.wait()

    @pl.loop(0, rows + 1)
    def _(n):
        @pl.when(n < rows)
        def _():
            filter_row(lax.rem(n + 2, rows))

        @pl.when(n > 0)
        def _():
            sketch_row(lax.rem(n + 1, rows))

    half = part.shape[1] // 2
    split = part[...].reshape(spaces, span // spaces, 2 * half)
    offered[...] = jnp.concatenate([split[:, :, :half], split[:, :, half:]], axis=1).astype(jnp.bfloat16)

    @pl.loop(1, spaces)
    def _(q):
        to, _ = across(q)
        pltpu.make_async_remote_copy(
            src_ref=offered.at[to],
            dst_ref=arrived.at[q - 1],
            send_sem=sum_sem.at[0],
            recv_sem=sum_sem.at[1],
            device_id=across(q),
            device_id_type=MESH,
        ).start()

    near = part[pl.ds(pl.multiple_of(s * 8, 8), 8), :]
    pltpu.make_async_copy(arrived, arrived, sum_sem.at[1]).wait()
    total = jnp.concatenate([near[:, :half], near[:, half:]], axis=0)
    for q in range(spaces - 1):
        total = total + arrived[q].astype(F32)
    own_ref[:, :half] = total[:8]
    own_ref[:, half:] = total[8:]
    mine_ref[...] = total.astype(jnp.bfloat16)
    all_ref[core, mine] = total.astype(jnp.bfloat16)

    @pl.loop(1, flat)
    def _(e):
        pltpu.make_async_remote_copy(
            src_ref=mine_ref,
            dst_ref=all_ref.at[core, mine],
            send_sem=gather_sem.at[0],
            recv_sem=gather_sem.at[1],
            device_id=around(e),
            device_id_type=MESH,
        ).start()

    others = all_ref.at[core, pl.ds(0, flat - 1)]
    pltpu.make_async_copy(others, others, gather_sem.at[1]).wait()
    pair = pltpu.make_async_remote_copy(
        src_ref=all_ref.at[core],
        dst_ref=all_ref.at[core],
        send_sem=pair_sem.at[0],
        recv_sem=pair_sem.at[1],
        device_id=(2 * chip + 1 - core, t),
        device_id_type=MESH,
    )
    pair.start()
    pltpu.make_async_copy(arrived, arrived, sum_sem.at[0]).wait()
    pltpu.make_async_copy(others, others, gather_sem.at[0]).wait()

    @pl.when(s < spaces - 1)
    def _():
        up.wait_send()

    @pl.when(s > 0)
    def _():
        down.wait_send()

    for i in range(rows):
        before, after = rims(i)

        @pl.when(t < blocks - 1)
        def _():
            before.wait_send()

        @pl.when(t > 0)
        def _():
            after.wait_send()

        pltpu.make_async_copy(heard.at[i], heard.at[i], energy_out.at[i]).wait()

    pair.wait()


def front(field, sketch, spaces, blocks):
    rows, lon, span = field.shape
    n = sketch.shape[2]
    piece = 144
    vmem = pl.BlockSpec(memory_space=pltpu.VMEM)
    hbm = pl.BlockSpec(memory_space=pl.ANY)
    return pl.pallas_call(
        functools.partial(front_kernel, span * blocks),
        out_shape=(
            jax.ShapeDtypeStruct((2, spaces // 2 * blocks, 16, n // 2), jnp.bfloat16),
            jax.ShapeDtypeStruct((8, n), F32),
        ),
        in_specs=[hbm, hbm, vmem, vmem],
        out_specs=(vmem, vmem),
        scratch_shapes=[
            pltpu.VMEM((rows + 4, lon + 32, span), jnp.bfloat16),
            pltpu.VMEM((rows, lon, span + 256), jnp.bfloat16),
            pltpu.VMEM((rows, lon, n), jnp.bfloat16),
            pltpu.VMEM((rows, span, lon), jnp.bfloat16),
            pltpu.VMEM((rows, 1, lon), F32),
            pltpu.VMEM((rows, blocks - 1, 1, lon), F32),
            pltpu.SemaphoreType.DMA((3,)),
            pltpu.SemaphoreType.DMA,
            pltpu.SemaphoreType.DMA((4,)),
            pltpu.SemaphoreType.DMA((4, rows)),
            pltpu.SemaphoreType.DMA((rows,)),
            pltpu.SemaphoreType.DMA((rows,)),
            pltpu.VMEM((span, n), F32),
            pltpu.VMEM((spaces, 16, n // 2), jnp.bfloat16),
            pltpu.VMEM((spaces - 1, 16, n // 2), jnp.bfloat16),
            pltpu.VMEM((16, n // 2), jnp.bfloat16),
            pltpu.SemaphoreType.DMA((2,)),
            pltpu.SemaphoreType.DMA((2,)),
            pltpu.SemaphoreType.DMA((2,)),
        ],
        compiler_params=pltpu.CompilerParams(
            collective_id=0, has_side_effects=True, vmem_limit_bytes=56 * 2**20
        ),
        name="front",
    )(field, sketch, jnp.asarray(band_weights(span)), jnp.asarray(ring_weights(piece)))


def factor_block(m_ref):
    lane8 = lax.broadcasted_iota(jnp.int32, (8, 1), 0)
    for q in range(16):
        top = 8 * q
        p = m_ref[top:top + 8, :]
        cols = [jnp.broadcast_to(m_ref[top:128, top + k:top + k + 1], (128 - top, 128)) for k in range(8)]
        scaled = []
        for k in range(8):
            c = cols[k]
            d = c[k:k + 1, :]
            r = 1.0 / d
            for m in range(k + 1, 8):
                cols[m] = cols[m] - c * (cols[m][k:k + 1, :] * r)
            row = p[k:k + 1, :]
            t = row * jnp.concatenate([r, r], axis=1)
            below = jnp.where(lane8 > k, c[0:8, :], 0.0)
            p = p - jnp.concatenate([below, below], axis=1) * t
            scaled.append(t)
            s = lax.rsqrt(d)
            m_ref[top + k:top + k + 1, :] = row * jnp.concatenate([s, s], axis=1)
        if q < 15:
            left = m_ref[top + 8:128, 0:128]
            right = m_ref[top + 8:128, 128:256]
            for k in range(8):
                c = cols[k][8:, :]
                left = left - c * scaled[k][:, 0:128]
                right = right - c * scaled[k][:, 128:256]
            m_ref[top + 8:128, 0:128] = left
            m_ref[top + 8:128, 128:256] = right

def factor_kernel(root, y_ref, own_ref, basis_ref, r_ref, a_ref, m_ref, rest_ref):
    n = own_ref.shape[1]
    blocks = n // 128
    pairs = y_ref[...].astype(F32)
    y = jnp.concatenate([pairs[:, :8].reshape(-1, n // 2), pairs[:, 8:].reshape(-1, n // 2)], axis=1).astype(jnp.bfloat16)
    a_ref[...] = lax.dot_general(y, y, (((0,), (0,)), ((), ())), preferred_element_type=F32)
    rest_ref[...] = own_ref[...]
    row = lax.broadcasted_iota(jnp.int32, (128, 128), 0)
    col = lax.broadcasted_iota(jnp.int32, (128, 128), 1)

    @pl.loop(0, blocks)
    def _(b):
        here = pl.ds(pl.multiple_of(b * 128, 128), 128)
        m_ref[:, 0:128] = a_ref[here, here]
        m_ref[:, 128:256] = (row == col).astype(F32)
        factor_block(m_ref)
        inv = m_ref[:, 128:256]
        x = lax.dot_general(rest_ref[:, here], inv, (((1,), (1,)), ((), ())), precision=HI, preferred_element_type=F32)
        basis_ref[:, here] = x * root
        panel = jnp.dot(inv, a_ref[here, :], precision=HI, preferred_element_type=F32)
        wide = lax.broadcasted_iota(jnp.int32, (128, n), 1) >= (b + 1) * 128
        panel = jnp.where(wide, panel, 0.0)
        r_ref[here, :] = panel * (1.0 / root)
        r_ref[here, here] = jnp.where(row <= col, m_ref[:, 0:128], 0.0) * (1.0 / root)
        rest_ref[...] -= jnp.dot(x, panel, precision=HI, preferred_element_type=F32)
        a_ref[...] -= lax.dot_general(panel, panel, (((0,), (0,)), ((), ())), precision=HI, preferred_element_type=F32)

def factor(y, own, hours):
    n = own.shape[1]
    return pl.pallas_call(
        functools.partial(factor_kernel, math.sqrt(hours)),
        out_shape=(jax.ShapeDtypeStruct((own.shape[0], n), F32), jax.ShapeDtypeStruct((n, n), F32)),
        in_specs=[pl.BlockSpec(memory_space=pltpu.VMEM)] * 2,
        out_specs=(pl.BlockSpec(memory_space=pltpu.VMEM), pl.BlockSpec(memory_space=pltpu.VMEM)),
        scratch_shapes=[pltpu.VMEM((n, n), F32), pltpu.VMEM((128, 256), F32), pltpu.VMEM((own.shape[0], n), F32)],
        compiler_params=pltpu.CompilerParams(vmem_limit_bytes=32 * 2**20),
        name="factor",
    )(y, own)


def body(field, sketch):
    spaces, blocks = lax.axis_size("space"), lax.axis_size("tm")
    all_hours = field.shape[2] * blocks
    everyone, own = front(field, sketch, spaces, blocks)
    return factor(everyone.reshape(-1, 16, everyone.shape[3]), own, all_hours)


def solution(mesh):
    placed = (P("space", None, "tm"), P("space", None, None))
    return jax.shard_map(
        body, mesh=mesh, in_specs=placed, out_specs=(P(("tm", "space"), None), P()), check_vma=False
    )
```

```python
import functools
import math

import jax
import jax.numpy as jnp
import numpy as np
from jax import lax
from jax.experimental import pallas as pl
from jax.experimental.pallas import tpu as pltpu
from jax.sharding import PartitionSpec as P

HALO = 120
F32 = jnp.float32
HI = lax.Precision.HIGHEST
MESH = pl.DeviceIdType.MESH
LAG = 4


low_cutoff = 1.0 / 240.0
high_cutoff = 0.4
smooth_taps = (1.0 / 16.0, 4.0 / 16.0, 6.0 / 16.0, 4.0 / 16.0, 1.0 / 16.0)


def band_weights(span):
    m = np.arange(span + 256, dtype=np.float64)[None, :] - 128.0 - np.arange(span, dtype=np.float64)[:, None]
    value = 2.0 * high_cutoff * np.sinc(2.0 * high_cutoff * m) - 2.0 * low_cutoff * np.sinc(2.0 * low_cutoff * m)
    value = value * np.sinc(m / (HALO + 1.0))
    return np.where(np.abs(m) <= HALO, value, 0.0).astype(np.float32).astype(jnp.bfloat16)


def ring_weights(piece):
    offset = np.arange(piece + 32)[None, :] - 16 - np.arange(piece)[:, None]
    value = np.zeros(offset.shape, np.float32)
    for shift in range(-2, 3):
        value = np.where(offset == shift, smooth_taps[shift + 2], value)
    return value.astype(jnp.bfloat16)


def front_kernel(
    hours,
    field_ref,
    sketch_ref,
    band_ref,
    ring_ref,
    all_ref,
    own_ref,
    x,
    series,
    omega,
    filtered,
    energy,
    heard,
    part,
    offered,
    arrived,
    mine_ref,
    load_sem,
    omega_sem,
    row_sem,
    rim_sem,
    energy_sem,
    sum_sem,
    sent_sem,
    gather_sem,
    pair_sem,
):
    spaces, blocks = lax.axis_size("space"), lax.axis_size("tm")
    s, t = lax.axis_index("space"), lax.axis_index("tm")
    rows, lon, span = field_ref.shape
    piece = ring_ref.shape[0]
    reach = lon // 2
    units = 2 * rows
    last = rows + 2
    chips = spaces // 2
    core, chip = lax.rem(s, 2), s // 2
    flat = chips * blocks
    mine = t * chips + chip

    def across(q):
        return lax.rem(s + q, spaces), t

    def around(e):
        to = lax.rem(mine + e, flat)
        return 2 * lax.rem(to, chips) + core, to // chips

    barrier = pltpu.get_barrier_semaphore()

    own = pltpu.make_async_copy(field_ref, x.at[2:last, 16 : lon + 16], load_sem.at[0])
    left = pltpu.make_async_copy(field_ref.at[:, lon - 16 : lon], x.at[2:last, 0:16], load_sem.at[1])
    right = pltpu.make_async_copy(field_ref.at[:, 0:16], x.at[2:last, lon + 16 : lon + 32], load_sem.at[2])
    own.start()
    left.start()
    right.start()
    load_omega = pltpu.make_async_copy(sketch_ref, omega, omega_sem)

    @pl.loop(1, spaces)
    def _(q):
        pl.semaphore_signal(barrier, inc=1, device_id=across(q), device_id_type=MESH)

    @pl.loop(1, flat)
    def _(e):
        pl.semaphore_signal(barrier, inc=1, device_id=around(e), device_id_type=MESH)

    def halo(part_of, step):
        take = slice(rows - 2, rows) if step > 0 else slice(0, 2)
        give = slice(0, 2) if step > 0 else slice(last, last + 2)
        if part_of == 0:
            wrap, inner = (lon - 16, 0), (0, reach + 16)
        else:
            wrap, inner = (0, lon + 16), (reach + 16, lon)
        sems = 2 * part_of + (0 if step > 0 else 1)
        copies = []
        for low, high, to in (
            (inner[0], inner[1], inner[0] + 16),
            (wrap[0], wrap[0] + 16, wrap[1]),
        ):
            copies.append(
                pltpu.make_async_remote_copy(
                    src_ref=field_ref.at[take, low:high],
                    dst_ref=x.at[give, to : to + high - low],
                    send_sem=row_sem.at[0, sems],
                    recv_sem=row_sem.at[1, sems],
                    device_id=(s + step, t),
                    device_id_type=MESH,
                )
            )
        return copies

    def halo_wait(part_of, step, side):
        give = slice(0, 2) if step > 0 else slice(last, last + 2)
        cut = reach + 32
        whole = x.at[give, 0:cut] if part_of == 0 else x.at[give, cut : lon + 32]
        sems = 2 * part_of + (0 if step > 0 else 1)
        pltpu.make_async_copy(whole, whole, row_sem.at[side, sems]).wait()

    def smooth(first, half):
        @pl.loop(0, reach // piece)
        def _(c):
            at = pl.multiple_of(half * reach + c * piece, 16)
            horizontal = [
                jnp.dot(ring_ref[...], x[first + r, pl.ds(at, piece + 32), :], preferred_element_type=F32)
                for r in range(6)
            ]
            for r in range(2):
                total = smooth_taps[2] * horizontal[r + 2] + smooth_taps[1] * (horizontal[r + 1] + horizontal[r + 3])
                total = total + smooth_taps[0] * (horizontal[r] + horizontal[r + 4])
                series[first + r, pl.ds(at, piece), 128 : 128 + span] = total.astype(jnp.bfloat16)

    def place(u):
        early = u < 4
        half = jnp.where(early, u // 2, (u - 4) // 4)
        row = jnp.where(early, 2 + lax.rem(u, 2), lax.rem(u, 4) + 4 - 6 * (lax.rem(u, 4) // 2))
        return row, pl.ds(pl.multiple_of(half * reach, 16), reach)

    def rims(u):
        row, where = place(u)
        before = pltpu.make_async_remote_copy(
            src_ref=series.at[row, where, span : span + 128],
            dst_ref=series.at[row, where, 0:128],
            send_sem=rim_sem.at[0, u],
            recv_sem=rim_sem.at[1, u],
            device_id=(s, t + 1),
            device_id_type=MESH,
        )
        after = pltpu.make_async_remote_copy(
            src_ref=series.at[row, where, 128:256],
            dst_ref=series.at[row, where, span + 128 : span + 256],
            send_sem=rim_sem.at[2, u],
            recv_sem=rim_sem.at[3, u],
            device_id=(s, t - 1),
            device_id_type=MESH,
        )
        return before, after

    def send_rims(u):
        before, after = rims(u)

        @pl.when(t < blocks - 1)
        def _():
            before.start()

        @pl.when(t > 0)
        def _():
            after.start()

    def sent_rims(u):
        before, after = rims(u)

        @pl.when(t < blocks - 1)
        def _():
            before.wait_send()

        @pl.when(t > 0)
        def _():
            after.wait_send()

    def filter_unit(u):
        row, where = place(u)
        before, after = rims(u)

        @pl.when(t > 0)
        def _():
            before.wait_recv()

        @pl.when(t < blocks - 1)
        def _():
            after.wait_recv()

        value = lax.dot_general(
            band_ref[...], series[row, where, :], (((1,), (1,)), ((), ())), preferred_element_type=F32
        ).astype(jnp.bfloat16)
        filtered[u] = value
        wide = value.astype(F32)
        energy[u] = jnp.sum(wide * wide, axis=0, keepdims=True)
        for q in range(1, blocks):
            pltpu.make_async_remote_copy(
                src_ref=energy.at[u],
                dst_ref=heard.at[u, q - 1],
                send_sem=energy_sem.at[0, u],
                recv_sem=energy_sem.at[1, u],
                device_id=(s, lax.rem(t + q, blocks)),
                device_id_type=MESH,
            ).start()

    def sketch_unit(u):
        row, where = place(u)
        pltpu.make_async_copy(heard.at[u], heard.at[u], energy_sem.at[1, u]).wait()
        total = energy[u]
        for q in range(blocks - 1):
            total = total + heard[u, q]
        inverse = lax.rsqrt(total / hours + 1e-06)
        standard = (filtered[u].astype(F32) * inverse).astype(jnp.bfloat16)
        part[...] += jnp.dot(standard, omega[row, where, :], preferred_element_type=F32)

    own.wait()
    left.wait()
    right.wait()
    smooth(2, 0)
    pl.semaphore_wait(barrier, spaces + flat - 2)

    for part_of in range(2):
        for step in (1, -1):
            copies = halo(part_of, step)

            @pl.when((s < spaces - 1) if step > 0 else (s > 0))
            def _():
                for copy in copies:
                    copy.start()

    send_rims(0)
    send_rims(1)
    smooth(2, 1)
    load_omega.start()

    @pl.when(s == spaces - 1)
    def _():
        x[last : last + 2] = jnp.zeros((2, lon + 32, span), jnp.bfloat16)

    @pl.when(s == 0)
    def _():
        x[0:2] = jnp.zeros((2, lon + 32, span), jnp.bfloat16)

    @pl.when(t == 0)
    def _():
        series[:, :, 0:128] = jnp.zeros((rows, lon, 128), jnp.bfloat16)

    @pl.when(t == blocks - 1)
    def _():
        series[:, :, span + 128 : span + 256] = jnp.zeros((rows, lon, 128), jnp.bfloat16)

    part[...] = jnp.zeros(part.shape, F32)
    load_omega.wait()

    @pl.loop(2, units + LAG)
    def _(n):
        for part_of in range(2):

            @pl.when(n == 4 + 4 * part_of)
            def _():
                @pl.when(s < spaces - 1)
                def _():
                    halo_wait(part_of, -1, 1)

                @pl.when(s > 0)
                def _():
                    halo_wait(part_of, 1, 1)

        @pl.when((n == 4) | (n == 8))
        def _():
            @pl.loop(0, 2)
            def _(k):
                smooth(4 - 4 * k, (n - 4) // 4)

        @pl.when(n < units)
        def _():
            sent_rims(n - 2)
            send_rims(n)

        @pl.when(n < units + 2)
        def _():
            filter_unit(n - 2)

        @pl.when(n >= LAG)
        def _():
            sketch_unit(n - LAG)

    half = part.shape[1] // 2
    split = part[...].reshape(spaces, span // spaces, 2 * half)
    offered[...] = jnp.concatenate([split[:, :, :half], split[:, :, half:]], axis=1).astype(jnp.bfloat16)

    @pl.loop(1, spaces)
    def _(q):
        to, _ = across(q)
        pltpu.make_async_remote_copy(
            src_ref=offered.at[to],
            dst_ref=arrived.at[q - 1],
            send_sem=sum_sem.at[0],
            recv_sem=sum_sem.at[1],
            device_id=across(q),
            device_id_type=MESH,
        ).start()

    near = part[pl.ds(pl.multiple_of(s * 8, 8), 8), :]
    pltpu.make_async_copy(arrived, arrived, sum_sem.at[1]).wait()
    total = jnp.concatenate([near[:, :half], near[:, half:]], axis=0)
    for q in range(spaces - 1):
        total = total + arrived[q].astype(F32)
    own_ref[:, :half] = total[:8]
    own_ref[:, half:] = total[8:]
    mine_ref[...] = total.astype(jnp.bfloat16)
    pltpu.make_async_copy(mine_ref, all_ref.at[core, t, chip], gather_sem.at[t]).start()

    @pl.loop(1, flat)
    def _(e):
        pltpu.make_async_remote_copy(
            src_ref=mine_ref,
            dst_ref=all_ref.at[core, t, chip],
            send_sem=sent_sem,
            recv_sem=gather_sem.at[t],
            device_id=around(e),
            device_id_type=MESH,
        ).start()

    def pair(k):
        group = all_ref.at[core, lax.rem(t + blocks - k, blocks)]
        return pltpu.make_async_remote_copy(
            src_ref=group,
            dst_ref=group,
            send_sem=pair_sem.at[0, k],
            recv_sem=pair_sem.at[1, k],
            device_id=(2 * chip + 1 - core, t),
            device_id_type=MESH,
        )

    for k in range(blocks):
        sender = lax.rem(t + blocks - k, blocks)
        group = all_ref.at[core, sender]
        pltpu.make_async_copy(group, group, gather_sem.at[sender]).wait()
        pair(k).start()

    for part_of in range(2):
        for step in (1, -1):

            @pl.when((s < spaces - 1) if step > 0 else (s > 0))
            def _():
                halo_wait(part_of, step, 0)

    sent_rims(units - 2)
    sent_rims(units - 1)

    @pl.loop(0, units)
    def _(u):
        pltpu.make_async_copy(heard.at[u], heard.at[u], energy_sem.at[0, u]).wait()

    pltpu.make_async_copy(arrived, arrived, sum_sem.at[0]).wait()
    for k in range(blocks):
        whole = all_ref.at[core, k] if k else all_ref.at[core, k, pl.ds(0, chips - 1)]
        pltpu.make_async_copy(whole, whole, sent_sem).wait()
    for k in range(blocks):
        pair(k).wait()


def front(field, sketch, spaces, blocks):
    rows, lon, span = field.shape
    n = sketch.shape[2]
    piece, chips, units = 144, spaces // 2, 2 * rows
    vmem = pl.BlockSpec(memory_space=pltpu.VMEM)
    hbm = pl.BlockSpec(memory_space=pl.ANY)
    return pl.pallas_call(
        functools.partial(front_kernel, span * blocks),
        out_shape=(
            jax.ShapeDtypeStruct((2, blocks, chips, 16, n // 2), jnp.bfloat16),
            jax.ShapeDtypeStruct((8, n), F32),
        ),
        in_specs=[hbm, hbm, vmem, vmem],
        out_specs=(vmem, vmem),
        scratch_shapes=[
            pltpu.VMEM((rows + 4, lon + 32, span), jnp.bfloat16),
            pltpu.VMEM((rows, lon, span + 256), jnp.bfloat16),
            pltpu.VMEM((rows, lon, n), jnp.bfloat16),
            pltpu.VMEM((units, span, lon // 2), jnp.bfloat16),
            pltpu.VMEM((units, 1, lon // 2), F32),
            pltpu.VMEM((units, blocks - 1, 1, lon // 2), F32),
            pltpu.VMEM((span, n), F32),
            pltpu.VMEM((spaces, 16, n // 2), jnp.bfloat16),
            pltpu.VMEM((spaces - 1, 16, n // 2), jnp.bfloat16),
            pltpu.VMEM((16, n // 2), jnp.bfloat16),
            pltpu.SemaphoreType.DMA((3,)),
            pltpu.SemaphoreType.DMA,
            pltpu.SemaphoreType.DMA((2, 4)),
            pltpu.SemaphoreType.DMA((4, units)),
            pltpu.SemaphoreType.DMA((2, units)),
            pltpu.SemaphoreType.DMA((2,)),
            pltpu.SemaphoreType.DMA,
            pltpu.SemaphoreType.DMA((blocks,)),
            pltpu.SemaphoreType.DMA((2, blocks)),
        ],
        compiler_params=pltpu.CompilerParams(
            collective_id=0, has_side_effects=True, vmem_limit_bytes=56 * 2**20
        ),
        name="front",
    )(field, sketch, jnp.asarray(band_weights(span)), jnp.asarray(ring_weights(piece)))


def factor_block(m_ref):
    lane8 = lax.broadcasted_iota(jnp.int32, (8, 1), 0)
    for q in range(16):
        top = 8 * q
        p = m_ref[top:top + 8, :]
        cols = [jnp.broadcast_to(m_ref[top:128, top + k:top + k + 1], (128 - top, 128)) for k in range(8)]
        scaled = []
        for k in range(8):
            c = cols[k]
            d = c[k:k + 1, :]
            r = 1.0 / d
            for m in range(k + 1, 8):
                cols[m] = cols[m] - c * (cols[m][k:k + 1, :] * r)
            row = p[k:k + 1, :]
            t = row * jnp.concatenate([r, r], axis=1)
            below = jnp.where(lane8 > k, c[0:8, :], 0.0)
            p = p - jnp.concatenate([below, below], axis=1) * t
            scaled.append(t)
            s = lax.rsqrt(d)
            m_ref[top + k:top + k + 1, :] = row * jnp.concatenate([s, s], axis=1)
        if q < 15:
            left = m_ref[top + 8:128, 0:128]
            right = m_ref[top + 8:128, 128:256]
            for k in range(8):
                c = cols[k][8:, :]
                left = left - c * scaled[k][:, 0:128]
                right = right - c * scaled[k][:, 128:256]
            m_ref[top + 8:128, 0:128] = left
            m_ref[top + 8:128, 128:256] = right

def factor_kernel(root, y_ref, own_ref, basis_ref, r_ref, a_ref, m_ref, rest_ref):
    n = own_ref.shape[1]
    blocks = n // 128
    pairs = y_ref[...].astype(F32)
    y = jnp.concatenate([pairs[:, :8].reshape(-1, n // 2), pairs[:, 8:].reshape(-1, n // 2)], axis=1).astype(jnp.bfloat16)
    a_ref[...] = lax.dot_general(y, y, (((0,), (0,)), ((), ())), preferred_element_type=F32)
    rest_ref[...] = own_ref[...]
    row = lax.broadcasted_iota(jnp.int32, (128, 128), 0)
    col = lax.broadcasted_iota(jnp.int32, (128, 128), 1)

    @pl.loop(0, blocks)
    def _(b):
        here = pl.ds(pl.multiple_of(b * 128, 128), 128)
        m_ref[:, 0:128] = a_ref[here, here]
        m_ref[:, 128:256] = (row == col).astype(F32)
        factor_block(m_ref)
        inv = m_ref[:, 128:256]
        x = lax.dot_general(rest_ref[:, here], inv, (((1,), (1,)), ((), ())), precision=HI, preferred_element_type=F32)
        basis_ref[:, here] = x * root
        panel = jnp.dot(inv, a_ref[here, :], precision=HI, preferred_element_type=F32)
        wide = lax.broadcasted_iota(jnp.int32, (128, n), 1) >= (b + 1) * 128
        panel = jnp.where(wide, panel, 0.0)
        r_ref[here, :] = panel * (1.0 / root)
        r_ref[here, here] = jnp.where(row <= col, m_ref[:, 0:128], 0.0) * (1.0 / root)
        rest_ref[...] -= jnp.dot(x, panel, precision=HI, preferred_element_type=F32)
        a_ref[...] -= lax.dot_general(panel, panel, (((0,), (0,)), ((), ())), precision=HI, preferred_element_type=F32)

def factor(y, own, hours):
    n = own.shape[1]
    return pl.pallas_call(
        functools.partial(factor_kernel, math.sqrt(hours)),
        out_shape=(jax.ShapeDtypeStruct((own.shape[0], n), F32), jax.ShapeDtypeStruct((n, n), F32)),
        in_specs=[pl.BlockSpec(memory_space=pltpu.VMEM)] * 2,
        out_specs=(pl.BlockSpec(memory_space=pltpu.VMEM), pl.BlockSpec(memory_space=pltpu.VMEM)),
        scratch_shapes=[pltpu.VMEM((n, n), F32), pltpu.VMEM((128, 256), F32), pltpu.VMEM((own.shape[0], n), F32)],
        compiler_params=pltpu.CompilerParams(vmem_limit_bytes=32 * 2**20),
        name="factor",
    )(y, own)


def body(field, sketch):
    spaces, blocks = lax.axis_size("space"), lax.axis_size("tm")
    all_hours = field.shape[2] * blocks
    everyone, own = front(field, sketch, spaces, blocks)
    return factor(everyone.reshape(-1, 16, everyone.shape[4]), own, all_hours)


def solution(mesh):
    placed = (P("space", None, "tm"), P("space", None, None))
    return jax.shard_map(
        body, mesh=mesh, in_specs=placed, out_specs=(P(("tm", "space"), None), P()), check_vma=False
    )
```

```python
import functools
import math

import jax
import jax.numpy as jnp
import numpy as np
from jax import lax
from jax.experimental import pallas as pl
from jax.experimental.pallas import tpu as pltpu
from jax.sharding import PartitionSpec as P

HALO = 120
F32 = jnp.float32
HI = lax.Precision.HIGH
MESH = pl.DeviceIdType.MESH
LAG = 4


low_cutoff = 1.0 / 240.0
high_cutoff = 0.4
smooth_taps = (1.0 / 16.0, 4.0 / 16.0, 6.0 / 16.0, 4.0 / 16.0, 1.0 / 16.0)


def band_weights(span):
    m = np.arange(span + 256, dtype=np.float64)[None, :] - 128.0 - np.arange(span, dtype=np.float64)[:, None]
    value = 2.0 * high_cutoff * np.sinc(2.0 * high_cutoff * m) - 2.0 * low_cutoff * np.sinc(2.0 * low_cutoff * m)
    value = value * np.sinc(m / (HALO + 1.0))
    return np.where(np.abs(m) <= HALO, value, 0.0).astype(np.float32).astype(jnp.bfloat16)


def ring_weights(piece):
    offset = np.arange(piece + 32)[None, :] - 16 - np.arange(piece)[:, None]
    value = np.zeros(offset.shape, np.float32)
    for shift in range(-2, 3):
        value = np.where(offset == shift, smooth_taps[shift + 2], value)
    return value.astype(jnp.bfloat16)


def front_kernel(
    hours,
    field_ref,
    sketch_ref,
    band_ref,
    ring_ref,
    all_ref,
    own_ref,
    x,
    series,
    omega,
    filtered,
    energy,
    heard,
    part,
    offered,
    arrived,
    mine_ref,
    ready,
    load_sem,
    omega_sem,
    row_sem,
    rim_sem,
    energy_sem,
    sum_sem,
    sent_sem,
    gather_sem,
    pair_sem,
):
    spaces, blocks = lax.axis_size("space"), lax.axis_size("tm")
    s, t = lax.axis_index("space"), lax.axis_index("tm")
    rows, lon, span = field_ref.shape
    piece = ring_ref.shape[0]
    reach = lon // 2
    units = 2 * rows
    last = rows + 2
    chips = spaces // 2
    core, chip = lax.rem(s, 2), s // 2
    flat = chips * blocks
    mine = t * chips + chip

    def across(q):
        return lax.rem(s + q, spaces), t

    def around(e):
        to = lax.rem(mine + e, flat)
        return 2 * lax.rem(to, chips) + core, to // chips

    barrier = pltpu.get_barrier_semaphore()

    own = pltpu.make_async_copy(field_ref, x.at[2:last, 16 : lon + 16], load_sem.at[0])
    left = pltpu.make_async_copy(field_ref.at[:, lon - 16 : lon], x.at[2:last, 0:16], load_sem.at[1])
    right = pltpu.make_async_copy(field_ref.at[:, 0:16], x.at[2:last, lon + 16 : lon + 32], load_sem.at[2])
    own.start()
    left.start()
    right.start()
    load_omega = pltpu.make_async_copy(sketch_ref, omega, omega_sem)

    def tell(semaphore, radius):
        for step in (radius, spaces - radius):
            pl.semaphore_signal(semaphore, inc=1, device_id=across(step), device_id_type=MESH)

    def tell_blocks(semaphore):
        for q in range(1, blocks):
            pl.semaphore_signal(semaphore, inc=1, device_id=(s, lax.rem(t + q, blocks)), device_id_type=MESH)

    tell(barrier, 1)
    tell_blocks(barrier)

    def halo(part_of, step):
        take = slice(rows - 2, rows) if step > 0 else slice(0, 2)
        give = slice(0, 2) if step > 0 else slice(last, last + 2)
        if part_of == 0:
            wrap, inner = (lon - 16, 0), (0, reach + 16)
        else:
            wrap, inner = (0, lon + 16), (reach + 16, lon)
        sems = 2 * part_of + (0 if step > 0 else 1)
        copies = []
        for low, high, to in (
            (inner[0], inner[1], inner[0] + 16),
            (wrap[0], wrap[0] + 16, wrap[1]),
        ):
            copies.append(
                pltpu.make_async_remote_copy(
                    src_ref=field_ref.at[take, low:high],
                    dst_ref=x.at[give, to : to + high - low],
                    send_sem=row_sem.at[0, sems],
                    recv_sem=row_sem.at[1, sems],
                    device_id=(s + step, t),
                    device_id_type=MESH,
                )
            )
        return copies

    def halo_wait(part_of, step, side):
        give = slice(0, 2) if step > 0 else slice(last, last + 2)
        cut = reach + 32
        whole = x.at[give, 0:cut] if part_of == 0 else x.at[give, cut : lon + 32]
        sems = 2 * part_of + (0 if step > 0 else 1)
        pltpu.make_async_copy(whole, whole, row_sem.at[side, sems]).wait()

    def smooth(first, half):
        @pl.loop(0, reach // piece)
        def _(c):
            at = pl.multiple_of(half * reach + c * piece, 16)
            horizontal = [
                jnp.dot(ring_ref[...], x[first + r, pl.ds(at, piece + 32), :], preferred_element_type=F32)
                for r in range(6)
            ]
            for r in range(2):
                total = smooth_taps[2] * horizontal[r + 2] + smooth_taps[1] * (horizontal[r + 1] + horizontal[r + 3])
                total = total + smooth_taps[0] * (horizontal[r] + horizontal[r + 4])
                series[first + r, pl.ds(at, piece), 128 : 128 + span] = total.astype(jnp.bfloat16)

    def place(u):
        early = u < 4
        half = jnp.where(early, u // 2, (u - 4) // 4)
        row = jnp.where(early, 2 + lax.rem(u, 2), lax.rem(u, 4) + 4 - 6 * (lax.rem(u, 4) // 2))
        return row, pl.ds(pl.multiple_of(half * reach, 16), reach)

    def rims(u):
        row, where = place(u)
        before = pltpu.make_async_remote_copy(
            src_ref=series.at[row, where, span : span + 128],
            dst_ref=series.at[row, where, 0:128],
            send_sem=rim_sem.at[0, u],
            recv_sem=rim_sem.at[1, u],
            device_id=(s, t + 1),
            device_id_type=MESH,
        )
        after = pltpu.make_async_remote_copy(
            src_ref=series.at[row, where, 128:256],
            dst_ref=series.at[row, where, span + 128 : span + 256],
            send_sem=rim_sem.at[2, u],
            recv_sem=rim_sem.at[3, u],
            device_id=(s, t - 1),
            device_id_type=MESH,
        )
        return before, after

    def send_rims(u):
        before, after = rims(u)

        @pl.when(t < blocks - 1)
        def _():
            before.start()

        @pl.when(t > 0)
        def _():
            after.start()

    def sent_rims(u):
        before, after = rims(u)

        @pl.when(t < blocks - 1)
        def _():
            before.wait_send()

        @pl.when(t > 0)
        def _():
            after.wait_send()

    def filter_unit(u):
        row, where = place(u)
        before, after = rims(u)

        @pl.when(t > 0)
        def _():
            before.wait_recv()

        @pl.when(t < blocks - 1)
        def _():
            after.wait_recv()

        value = lax.dot_general(
            band_ref[...], series[row, where, :], (((1,), (1,)), ((), ())), preferred_element_type=F32
        ).astype(jnp.bfloat16)
        filtered[u] = value
        wide = value.astype(F32)
        energy[u] = jnp.sum(wide * wide, axis=0, keepdims=True)
        for q in range(1, blocks):
            pltpu.make_async_remote_copy(
                src_ref=energy.at[u],
                dst_ref=heard.at[u, q - 1],
                send_sem=energy_sem.at[0, u],
                recv_sem=energy_sem.at[1, u],
                device_id=(s, lax.rem(t + q, blocks)),
                device_id_type=MESH,
            ).start()

    def sketch_unit(u):
        row, where = place(u)
        pltpu.make_async_copy(heard.at[u], heard.at[u], energy_sem.at[1, u]).wait()
        total = energy[u]
        for q in range(blocks - 1):
            total = total + heard[u, q]
        inverse = lax.rsqrt(total / hours + 1e-06)
        standard = (filtered[u].astype(F32) * inverse).astype(jnp.bfloat16)
        part[...] += jnp.dot(standard, omega[row, where, :], preferred_element_type=F32)

    own.wait()
    left.wait()
    right.wait()
    smooth(2, 0)
    pl.semaphore_wait(barrier, blocks + 1)

    for part_of in range(2):
        for step in (1, -1):
            copies = halo(part_of, step)

            @pl.when((s < spaces - 1) if step > 0 else (s > 0))
            def _():
                for copy in copies:
                    copy.start()

    send_rims(0)
    send_rims(1)
    smooth(2, 1)
    load_omega.start()

    @pl.when(s == spaces - 1)
    def _():
        x[last : last + 2] = jnp.zeros((2, lon + 32, span), jnp.bfloat16)

    @pl.when(s == 0)
    def _():
        x[0:2] = jnp.zeros((2, lon + 32, span), jnp.bfloat16)

    @pl.when(t == 0)
    def _():
        series[:, :, 0:128] = jnp.zeros((rows, lon, 128), jnp.bfloat16)

    @pl.when(t == blocks - 1)
    def _():
        series[:, :, span + 128 : span + 256] = jnp.zeros((rows, lon, 128), jnp.bfloat16)

    part[...] = jnp.zeros(part.shape, F32)
    load_omega.wait()

    @pl.loop(2, units + LAG)
    def _(n):
        for part_of in range(2):

            @pl.when(n == 4 + 4 * part_of)
            def _():
                @pl.when(s < spaces - 1)
                def _():
                    halo_wait(part_of, -1, 1)

                @pl.when(s > 0)
                def _():
                    halo_wait(part_of, 1, 1)

        @pl.when((n == 4) | (n == 8))
        def _():
            @pl.loop(0, 2)
            def _(k):
                smooth(4 - 4 * k, (n - 4) // 4)

        @pl.when(n < units)
        def _():
            sent_rims(n - 2)
            send_rims(n)

        for k in range(5):

            @pl.when(n == 5 + k)
            def _():
                if k:
                    pl.semaphore_wait(ready.at[k - 1], 2)
                if k < 4:
                    tell(ready.at[k], 2**k)
                else:
                    tell_blocks(ready.at[k])

        @pl.when(n < units + 2)
        def _():
            filter_unit(n - 2)

        @pl.when(n >= LAG)
        def _():
            sketch_unit(n - LAG)

    pl.semaphore_wait(ready.at[4], blocks - 1)
    half = part.shape[1] // 2
    split = part[...].reshape(spaces, span // spaces, 2 * half)
    offered[...] = jnp.concatenate([split[:, :, :half], split[:, :, half:]], axis=1).astype(jnp.bfloat16)

    @pl.loop(1, spaces)
    def _(q):
        to, _ = across(q)
        pltpu.make_async_remote_copy(
            src_ref=offered.at[to],
            dst_ref=arrived.at[q - 1],
            send_sem=sum_sem.at[0],
            recv_sem=sum_sem.at[1],
            device_id=across(q),
            device_id_type=MESH,
        ).start()

    near = part[pl.ds(pl.multiple_of(s * 8, 8), 8), :]
    pltpu.make_async_copy(arrived, arrived, sum_sem.at[1]).wait()
    total = jnp.concatenate([near[:, :half], near[:, half:]], axis=0)
    for q in range(spaces - 1):
        total = total + arrived[q].astype(F32)
    own_ref[:, :half] = total[:8]
    own_ref[:, half:] = total[8:]
    mine_ref[...] = total.astype(jnp.bfloat16)
    pltpu.make_async_copy(mine_ref, all_ref.at[core, t, chip], gather_sem.at[t]).start()

    @pl.loop(1, flat)
    def _(e):
        pltpu.make_async_remote_copy(
            src_ref=mine_ref,
            dst_ref=all_ref.at[core, t, chip],
            send_sem=sent_sem,
            recv_sem=gather_sem.at[t],
            device_id=around(e),
            device_id_type=MESH,
        ).start()

    def pair(k):
        group = all_ref.at[core, lax.rem(t + blocks - k, blocks)]
        return pltpu.make_async_remote_copy(
            src_ref=group,
            dst_ref=group,
            send_sem=pair_sem.at[0, k],
            recv_sem=pair_sem.at[1, k],
            device_id=(2 * chip + 1 - core, t),
            device_id_type=MESH,
        )

    for k in range(blocks):
        sender = lax.rem(t + blocks - k, blocks)
        group = all_ref.at[core, sender]
        pltpu.make_async_copy(group, group, gather_sem.at[sender]).wait()
        pair(k).start()

    for part_of in range(2):
        for step in (1, -1):

            @pl.when((s < spaces - 1) if step > 0 else (s > 0))
            def _():
                halo_wait(part_of, step, 0)

    sent_rims(units - 2)
    sent_rims(units - 1)

    @pl.loop(0, units)
    def _(u):
        pltpu.make_async_copy(heard.at[u], heard.at[u], energy_sem.at[0, u]).wait()

    pltpu.make_async_copy(arrived, arrived, sum_sem.at[0]).wait()
    for k in range(blocks):
        whole = all_ref.at[core, k] if k else all_ref.at[core, k, pl.ds(0, chips - 1)]
        pltpu.make_async_copy(whole, whole, sent_sem).wait()
    for k in range(blocks):
        pair(k).wait()


def front(field, sketch, spaces, blocks):
    rows, lon, span = field.shape
    n = sketch.shape[2]
    piece, chips, units = 144, spaces // 2, 2 * rows
    vmem = pl.BlockSpec(memory_space=pltpu.VMEM)
    hbm = pl.BlockSpec(memory_space=pl.ANY)
    return pl.pallas_call(
        functools.partial(front_kernel, span * blocks),
        out_shape=(
            jax.ShapeDtypeStruct((2, blocks, chips, 16, n // 2), jnp.bfloat16),
            jax.ShapeDtypeStruct((8, n), F32),
        ),
        in_specs=[hbm, hbm, vmem, vmem],
        out_specs=(vmem, vmem),
        scratch_shapes=[
            pltpu.VMEM((rows + 4, lon + 32, span), jnp.bfloat16),
            pltpu.VMEM((rows, lon, span + 256), jnp.bfloat16),
            pltpu.VMEM((rows, lon, n), jnp.bfloat16),
            pltpu.VMEM((units, span, lon // 2), jnp.bfloat16),
            pltpu.VMEM((units, 1, lon // 2), F32),
            pltpu.VMEM((units, blocks - 1, 1, lon // 2), F32),
            pltpu.VMEM((span, n), F32),
            pltpu.VMEM((spaces, 16, n // 2), jnp.bfloat16),
            pltpu.VMEM((spaces - 1, 16, n // 2), jnp.bfloat16),
            pltpu.VMEM((16, n // 2), jnp.bfloat16),
            pltpu.SemaphoreType.REGULAR((5,)),
            pltpu.SemaphoreType.DMA((3,)),
            pltpu.SemaphoreType.DMA,
            pltpu.SemaphoreType.DMA((2, 4)),
            pltpu.SemaphoreType.DMA((4, units)),
            pltpu.SemaphoreType.DMA((2, units)),
            pltpu.SemaphoreType.DMA((2,)),
            pltpu.SemaphoreType.DMA,
            pltpu.SemaphoreType.DMA((blocks,)),
            pltpu.SemaphoreType.DMA((2, blocks)),
        ],
        compiler_params=pltpu.CompilerParams(
            collective_id=0, has_side_effects=True, vmem_limit_bytes=56 * 2**20
        ),
        name="front",
    )(field, sketch, jnp.asarray(band_weights(span)), jnp.asarray(ring_weights(piece)))


def factor_block(m_ref):
    lane8 = lax.broadcasted_iota(jnp.int32, (8, 1), 0)
    for q in range(16):
        top = 8 * q
        p = m_ref[top:top + 8, :]
        cols = [jnp.broadcast_to(m_ref[top:128, top + k:top + k + 1], (128 - top, 128)) for k in range(8)]
        scaled = []
        for k in range(8):
            c = cols[k]
            d = c[k:k + 1, :]
            r = 1.0 / d
            for m in range(k + 1, 8):
                cols[m] = cols[m] - c * (cols[m][k:k + 1, :] * r)
            row = p[k:k + 1, :]
            t = row * jnp.concatenate([r, r], axis=1)
            below = jnp.where(lane8 > k, c[0:8, :], 0.0)
            p = p - jnp.concatenate([below, below], axis=1) * t
            scaled.append(t)
            s = lax.rsqrt(d)
            m_ref[top + k:top + k + 1, :] = row * jnp.concatenate([s, s], axis=1)
        if q < 15:
            left = m_ref[top + 8:128, 0:128]
            right = m_ref[top + 8:128, 128:256]
            for k in range(8):
                c = cols[k][8:, :]
                left = left - c * scaled[k][:, 0:128]
                right = right - c * scaled[k][:, 128:256]
            m_ref[top + 8:128, 0:128] = left
            m_ref[top + 8:128, 128:256] = right

def factor_kernel(root, y_ref, own_ref, basis_ref, r_ref, a_ref, m_ref, rest_ref):
    n = own_ref.shape[1]
    blocks = n // 128
    pairs = y_ref[...].astype(F32)
    y = jnp.concatenate([pairs[:, :8].reshape(-1, n // 2), pairs[:, 8:].reshape(-1, n // 2)], axis=1).astype(jnp.bfloat16)
    a_ref[...] = lax.dot_general(y, y, (((0,), (0,)), ((), ())), preferred_element_type=F32)
    rest_ref[...] = own_ref[...]
    row = lax.broadcasted_iota(jnp.int32, (128, 128), 0)
    col = lax.broadcasted_iota(jnp.int32, (128, 128), 1)

    @pl.loop(0, blocks)
    def _(b):
        here = pl.ds(pl.multiple_of(b * 128, 128), 128)
        m_ref[:, 0:128] = a_ref[here, here]
        m_ref[:, 128:256] = (row == col).astype(F32)
        factor_block(m_ref)
        inv = m_ref[:, 128:256]
        x = lax.dot_general(rest_ref[:, here], inv, (((1,), (1,)), ((), ())), precision=HI, preferred_element_type=F32)
        basis_ref[:, here] = x * root
        panel = jnp.dot(inv, a_ref[here, :], precision=HI, preferred_element_type=F32)
        wide = lax.broadcasted_iota(jnp.int32, (128, n), 1) >= (b + 1) * 128
        panel = jnp.where(wide, panel, 0.0)
        r_ref[here, :] = panel * (1.0 / root)
        r_ref[here, here] = jnp.where(row <= col, m_ref[:, 0:128], 0.0) * (1.0 / root)
        rest_ref[...] -= jnp.dot(x, panel, precision=HI, preferred_element_type=F32)
        a_ref[...] -= lax.dot_general(panel, panel, (((0,), (0,)), ((), ())), precision=HI, preferred_element_type=F32)

def factor(y, own, hours):
    n = own.shape[1]
    return pl.pallas_call(
        functools.partial(factor_kernel, math.sqrt(hours)),
        out_shape=(jax.ShapeDtypeStruct((own.shape[0], n), F32), jax.ShapeDtypeStruct((n, n), F32)),
        in_specs=[pl.BlockSpec(memory_space=pltpu.VMEM)] * 2,
        out_specs=(pl.BlockSpec(memory_space=pltpu.VMEM), pl.BlockSpec(memory_space=pltpu.VMEM)),
        scratch_shapes=[pltpu.VMEM((n, n), F32), pltpu.VMEM((128, 256), F32), pltpu.VMEM((own.shape[0], n), F32)],
        compiler_params=pltpu.CompilerParams(vmem_limit_bytes=32 * 2**20),
        name="factor",
    )(y, own)


def body(field, sketch):
    spaces, blocks = lax.axis_size("space"), lax.axis_size("tm")
    all_hours = field.shape[2] * blocks
    everyone, own = front(field, sketch, spaces, blocks)
    return factor(everyone.reshape(-1, 16, everyone.shape[4]), own, all_hours)


def solution(mesh):
    placed = (P("space", None, "tm"), P("space", None, None))
    return jax.shard_map(
        body, mesh=mesh, in_specs=placed, out_specs=(P(("tm", "space"), None), P()), check_vma=False
    )
```

```python
import functools
import math

import jax
import jax.numpy as jnp
import numpy as np
from jax import lax
from jax.experimental import pallas as pl
from jax.experimental.pallas import tpu as pltpu
from jax.sharding import PartitionSpec as P

HALO = 120
F32 = jnp.float32
HI = lax.Precision.HIGH
MESH = pl.DeviceIdType.MESH
LAG = 4


low_cutoff = 1.0 / 240.0
high_cutoff = 0.4
smooth_taps = (1.0 / 16.0, 4.0 / 16.0, 6.0 / 16.0, 4.0 / 16.0, 1.0 / 16.0)


def band_weights(span):
    m = np.arange(span + 256, dtype=np.float64)[None, :] - 128.0 - np.arange(span, dtype=np.float64)[:, None]
    value = 2.0 * high_cutoff * np.sinc(2.0 * high_cutoff * m) - 2.0 * low_cutoff * np.sinc(2.0 * low_cutoff * m)
    value = value * np.sinc(m / (HALO + 1.0))
    return np.where(np.abs(m) <= HALO, value, 0.0).astype(np.float32).astype(jnp.bfloat16)


def ring_weights(piece):
    offset = np.arange(piece + 32)[None, :] - 16 - np.arange(piece)[:, None]
    value = np.zeros(offset.shape, np.float32)
    for shift in range(-2, 3):
        value = np.where(offset == shift, smooth_taps[shift + 2], value)
    return value.astype(jnp.bfloat16)


def front_kernel(
    hours,
    field_ref,
    sketch_ref,
    band_ref,
    ring_ref,
    all_ref,
    own_ref,
    x,
    series,
    packed,
    omega,
    filtered,
    energy,
    heard,
    part,
    offered,
    arrived,
    mine_ref,
    ready,
    load_sem,
    omega_sem,
    row_sem,
    rim_sem,
    energy_sem,
    sum_sem,
    sent_sem,
    gather_sem,
    pair_sem,
):
    spaces, blocks = lax.axis_size("space"), lax.axis_size("tm")
    s, t = lax.axis_index("space"), lax.axis_index("tm")
    rows, lon, span = field_ref.shape
    piece = ring_ref.shape[0]
    reach = lon // 2
    units = 2 * rows
    last = rows + 2
    chips = spaces // 2
    core, chip = lax.rem(s, 2), s // 2

    def across(q):
        return lax.rem(s + q, spaces), t

    barrier = pltpu.get_barrier_semaphore()

    own = pltpu.make_async_copy(field_ref, x.at[2:last, 16 : lon + 16], load_sem.at[0])
    left = pltpu.make_async_copy(field_ref.at[:, lon - 16 : lon], x.at[2:last, 0:16], load_sem.at[1])
    right = pltpu.make_async_copy(field_ref.at[:, 0:16], x.at[2:last, lon + 16 : lon + 32], load_sem.at[2])
    own.start()
    left.start()
    right.start()
    load_omega = pltpu.make_async_copy(sketch_ref, omega, omega_sem)

    def tell(semaphore, radius):
        for step in (radius, spaces - radius):
            pl.semaphore_signal(semaphore, inc=1, device_id=across(step), device_id_type=MESH)

    def tell_blocks(semaphore):
        for q in range(1, blocks):
            pl.semaphore_signal(semaphore, inc=1, device_id=(s, lax.rem(t + q, blocks)), device_id_type=MESH)

    tell(barrier, 1)
    tell_blocks(barrier)

    def halo(part_of, step):
        take = slice(rows - 2, rows) if step > 0 else slice(0, 2)
        give = slice(0, 2) if step > 0 else slice(last, last + 2)
        if part_of == 0:
            wrap, inner = (lon - 16, 0), (0, reach + 16)
        else:
            wrap, inner = (0, lon + 16), (reach + 16, lon)
        sems = 2 * part_of + (0 if step > 0 else 1)
        copies = []
        for low, high, to in (
            (inner[0], inner[1], inner[0] + 16),
            (wrap[0], wrap[0] + 16, wrap[1]),
        ):
            copies.append(
                pltpu.make_async_remote_copy(
                    src_ref=field_ref.at[take, low:high],
                    dst_ref=x.at[give, to : to + high - low],
                    send_sem=row_sem.at[0, sems],
                    recv_sem=row_sem.at[1, sems],
                    device_id=(s + step, t),
                    device_id_type=MESH,
                )
            )
        return copies

    def halo_wait(part_of, step, side):
        give = slice(0, 2) if step > 0 else slice(last, last + 2)
        cut = reach + 32
        whole = x.at[give, 0:cut] if part_of == 0 else x.at[give, cut : lon + 32]
        sems = 2 * part_of + (0 if step > 0 else 1)
        pltpu.make_async_copy(whole, whole, row_sem.at[side, sems]).wait()

    def smooth(first, half):
        @pl.loop(0, reach // piece)
        def _(c):
            at = pl.multiple_of(half * reach + c * piece, 16)
            horizontal = [
                jnp.dot(ring_ref[...], x[first + r, pl.ds(at, piece + 32), :], preferred_element_type=F32)
                for r in range(6)
            ]
            for r in range(2):
                total = smooth_taps[2] * horizontal[r + 2] + smooth_taps[1] * (horizontal[r + 1] + horizontal[r + 3])
                total = total + smooth_taps[0] * (horizontal[r] + horizontal[r + 4])
                series[first + r, pl.ds(at, piece), 128 : 128 + span] = total.astype(jnp.bfloat16)

    def place(u):
        early = u < 4
        half = jnp.where(early, u // 2, (u - 4) // 4)
        row = jnp.where(early, 2 + lax.rem(u, 2), lax.rem(u, 4) + 4 - 6 * (lax.rem(u, 4) // 2))
        return row, pl.ds(pl.multiple_of(half * reach, 16), reach)

    keep = packed.shape[2]
    extra = reach - keep
    pieces = HALO // 8
    lane = lax.broadcasted_iota(jnp.int32, (extra, 128), 1)

    def within(where, start, size):
        return pl.ds(pl.multiple_of(where.start + start, 16), size)

    def pack(u):
        row, where = place(u)
        for side, low, spare in ((0, span, lane < 8), (1, 128, lane >= HALO)):
            tile = slice(low, low + 128)
            ending = series[row, within(where, keep, extra), tile].astype(F32)
            for k in range(pieces):
                at = k * extra
                same = series[row, within(where, at, extra), tile].astype(F32)
                moved = pltpu.roll(ending, HALO - 8 * k, 1)
                packed[side, lax.rem(u, 2), at : at + extra, :] = jnp.where(spare, moved, same).astype(jnp.bfloat16)
            at = pieces * extra
            packed[side, lax.rem(u, 2), at:keep, :] = series[row, within(where, at, keep - at), tile]

    def unpack(u):
        row, where = place(u)
        for low, first in ((0, 8), (span + 128, 0)):
            tile = slice(low, low + 128)
            ending = jnp.zeros((extra, 128), F32)
            for k in range(pieces):
                moved = pltpu.roll(series[row, within(where, k * extra, extra), tile].astype(F32), 8 + 8 * k, 1)
                at = first + 8 * k
                ending = jnp.where((lane >= at) & (lane < at + 8), moved, ending)
            series[row, within(where, keep, extra), tile] = ending.astype(jnp.bfloat16)

    def rims(u):
        row, where = place(u)
        before = pltpu.make_async_remote_copy(
            src_ref=packed.at[0, lax.rem(u, 2)],
            dst_ref=series.at[row, within(where, 0, keep), 0:128],
            send_sem=rim_sem.at[0, u],
            recv_sem=rim_sem.at[1, u],
            device_id=(s, t + 1),
            device_id_type=MESH,
        )
        after = pltpu.make_async_remote_copy(
            src_ref=packed.at[1, lax.rem(u, 2)],
            dst_ref=series.at[row, within(where, 0, keep), span + 128 : span + 256],
            send_sem=rim_sem.at[2, u],
            recv_sem=rim_sem.at[3, u],
            device_id=(s, t - 1),
            device_id_type=MESH,
        )
        return before, after

    def send_rims(u):
        pack(u)
        before, after = rims(u)

        @pl.when(t < blocks - 1)
        def _():
            before.start()

        @pl.when(t > 0)
        def _():
            after.start()

    def sent_rims(u):
        before, after = rims(u)

        @pl.when(t < blocks - 1)
        def _():
            before.wait_send()

        @pl.when(t > 0)
        def _():
            after.wait_send()

    def filter_unit(u):
        row, where = place(u)
        before, after = rims(u)

        @pl.when(t > 0)
        def _():
            before.wait_recv()

        @pl.when(t < blocks - 1)
        def _():
            after.wait_recv()

        unpack(u)
        value = lax.dot_general(
            band_ref[...], series[row, where, :], (((1,), (1,)), ((), ())), preferred_element_type=F32
        ).astype(jnp.bfloat16)
        filtered[u] = value
        wide = value.astype(F32)
        energy[u] = jnp.sum(wide * wide, axis=0, keepdims=True)
        for q in range(1, blocks):
            pltpu.make_async_remote_copy(
                src_ref=energy.at[u],
                dst_ref=heard.at[u, q - 1],
                send_sem=energy_sem.at[0, u],
                recv_sem=energy_sem.at[1, u],
                device_id=(s, lax.rem(t + q, blocks)),
                device_id_type=MESH,
            ).start()

    def sketch_unit(u):
        row, where = place(u)
        pltpu.make_async_copy(heard.at[u], heard.at[u], energy_sem.at[1, u]).wait()
        total = energy[u]
        for q in range(blocks - 1):
            total = total + heard[u, q]
        inverse = lax.rsqrt(total / hours + 1e-06)
        standard = (filtered[u].astype(F32) * inverse).astype(jnp.bfloat16)
        part[...] += jnp.dot(standard, omega[row, where, :], preferred_element_type=F32)

    own.wait()
    left.wait()
    right.wait()
    smooth(2, 0)
    pl.semaphore_wait(barrier, blocks + 1)

    for part_of in range(2):
        for step in (1, -1):
            copies = halo(part_of, step)

            @pl.when((s < spaces - 1) if step > 0 else (s > 0))
            def _():
                for copy in copies:
                    copy.start()

    @pl.loop(0, 2)
    def _(u):
        send_rims(u)

    smooth(2, 1)
    load_omega.start()

    @pl.when(s == spaces - 1)
    def _():
        x[last : last + 2] = jnp.zeros((2, lon + 32, span), jnp.bfloat16)

    @pl.when(s == 0)
    def _():
        x[0:2] = jnp.zeros((2, lon + 32, span), jnp.bfloat16)

    @pl.when(t == 0)
    def _():
        series[:, :, 0:128] = jnp.zeros((rows, lon, 128), jnp.bfloat16)

    @pl.when(t == blocks - 1)
    def _():
        series[:, :, span + 128 : span + 256] = jnp.zeros((rows, lon, 128), jnp.bfloat16)

    part[...] = jnp.zeros(part.shape, F32)
    load_omega.wait()

    @pl.loop(2, units + LAG)
    def _(n):
        for part_of in range(2):

            @pl.when(n == 4 + 4 * part_of)
            def _():
                @pl.when(s < spaces - 1)
                def _():
                    halo_wait(part_of, -1, 1)

                @pl.when(s > 0)
                def _():
                    halo_wait(part_of, 1, 1)

        @pl.when((n == 4) | (n == 8))
        def _():
            @pl.loop(0, 2)
            def _(k):
                smooth(4 - 4 * k, (n - 4) // 4)

        @pl.when(n < units)
        def _():
            sent_rims(n - 2)
            send_rims(n)

        for k in range(5):

            @pl.when(n == 5 + k)
            def _():
                if k:
                    pl.semaphore_wait(ready.at[k - 1], 2)
                if k < 4:
                    tell(ready.at[k], 2**k)
                else:
                    tell_blocks(ready.at[k])

        @pl.when(n < units + 2)
        def _():
            filter_unit(n - 2)

        @pl.when(n >= LAG)
        def _():
            sketch_unit(n - LAG)

    pl.semaphore_wait(ready.at[4], blocks - 1)
    half = part.shape[1] // 2
    split = part[...].reshape(spaces, span // spaces, 2 * half)
    offered[...] = jnp.concatenate([split[:, :, :half], split[:, :, half:]], axis=1).astype(jnp.bfloat16)

    @pl.loop(1, spaces)
    def _(q):
        to, _ = across(q)
        pltpu.make_async_remote_copy(
            src_ref=offered.at[to],
            dst_ref=arrived.at[q - 1],
            send_sem=sum_sem.at[0],
            recv_sem=sum_sem.at[1],
            device_id=across(q),
            device_id_type=MESH,
        ).start()

    near = part[pl.ds(pl.multiple_of(s * 8, 8), 8), :]
    pltpu.make_async_copy(arrived, arrived, sum_sem.at[1]).wait()
    total = jnp.concatenate([near[:, :half], near[:, half:]], axis=0)
    for q in range(spaces - 1):
        total = total + arrived[q].astype(F32)
    own_ref[:, :half] = total[:8]
    own_ref[:, half:] = total[8:]
    mine_ref[...] = total.astype(jnp.bfloat16)
    all_ref[core, t, chip] = total.astype(jnp.bfloat16)
    first, second = slice(0, half // 2), slice(half // 2, half)
    near_chips = chips // 4

    def block_peer(q):
        return s, lax.rem(t + q, blocks)

    def chip_peer(c):
        return 2 * lax.rem(chip + c, chips) + core, t

    def give(ref, to, kind, recv_sem, peer):
        pltpu.make_async_remote_copy(
            src_ref=ref,
            dst_ref=to,
            send_sem=sent_sem.at[kind],
            recv_sem=recv_sem,
            device_id=peer,
            device_id_type=MESH,
        ).start()

    def settle(ref, semaphore):
        pltpu.make_async_copy(ref, ref, semaphore).wait()

    for q in range(1, blocks):
        give(mine_ref.at[:, first], all_ref.at[core, t, chip, :, first], 0, gather_sem.at[0], block_peer(q))

    @pl.loop(1, chips)
    def _(c):
        give(mine_ref.at[:, second], all_ref.at[core, t, chip, :, second], 1, gather_sem.at[1], chip_peer(c))

    settle(all_ref.at[core, pl.ds(0, blocks - 1), chip, :, first], gather_sem.at[0])
    column = all_ref.at[core, :, chip, :, first]

    @pl.loop(1, chips)
    def _(c):
        give(column, column, 2, gather_sem.at[2 + chip // near_chips], chip_peer(c))

    settle(all_ref.at[core, t, pl.ds(0, chips - 1), :, second], gather_sem.at[1])
    plane = all_ref.at[core, t, :, :, second]
    for q in range(1, blocks):
        give(plane, plane, 3, gather_sem.at[5 + q], block_peer(q))

    def pair(k):
        j = k // 2
        if k % 2:
            group = all_ref.at[core, lax.rem(t + blocks - (0, 1, 3, 2)[j], blocks), :, :, second]
        else:
            at = lax.rem(chip // near_chips + j, 4) * near_chips
            group = all_ref.at[core, :, pl.ds(at, near_chips), :, first]
        return pltpu.make_async_remote_copy(
            src_ref=group,
            dst_ref=group,
            send_sem=pair_sem.at[0, k],
            recv_sem=pair_sem.at[1, k],
            device_id=(2 * chip + 1 - core, t),
            device_id_type=MESH,
        )

    for k in (1, 0, 3, 2, 5, 4, 7, 6):
        j = k // 2
        if k % 2:
            if j:
                settle(plane, gather_sem.at[5 + (0, 1, 3, 2)[j]])
        else:
            count = near_chips - 1 if j == 0 else near_chips
            settle(
                all_ref.at[core, :, pl.ds(0, count), :, first],
                gather_sem.at[2 + lax.rem(chip // near_chips + j, 4)],
            )
        pair(k).start()

    for part_of in range(2):
        for step in (1, -1):

            @pl.when((s < spaces - 1) if step > 0 else (s > 0))
            def _():
                halo_wait(part_of, step, 0)

    sent_rims(units - 2)
    sent_rims(units - 1)

    @pl.loop(0, units)
    def _(u):
        pltpu.make_async_copy(heard.at[u], heard.at[u], energy_sem.at[0, u]).wait()

    pltpu.make_async_copy(arrived, arrived, sum_sem.at[0]).wait()
    settle(all_ref.at[core, pl.ds(0, blocks - 1), chip, :, first], sent_sem.at[0])
    settle(all_ref.at[core, t, pl.ds(0, chips - 1), :, second], sent_sem.at[1])
    settle(all_ref.at[core, :, pl.ds(0, chips - 1), :, first], sent_sem.at[2])
    settle(all_ref.at[core, pl.ds(0, blocks - 1), :, :, second], sent_sem.at[3])
    for k in range(8):
        pair(k).wait()


def front(field, sketch, spaces, blocks):
    rows, lon, span = field.shape
    n = sketch.shape[2]
    piece, chips, units = 144, spaces // 2, 2 * rows
    keep = -(-lon * HALO // 4096) * 16
    vmem = pl.BlockSpec(memory_space=pltpu.VMEM)
    hbm = pl.BlockSpec(memory_space=pl.ANY)
    return pl.pallas_call(
        functools.partial(front_kernel, span * blocks),
        out_shape=(
            jax.ShapeDtypeStruct((2, blocks, chips, 16, n // 2), jnp.bfloat16),
            jax.ShapeDtypeStruct((8, n), F32),
        ),
        in_specs=[hbm, hbm, vmem, vmem],
        out_specs=(vmem, vmem),
        scratch_shapes=[
            pltpu.VMEM((rows + 4, lon + 32, span), jnp.bfloat16),
            pltpu.VMEM((rows, lon, span + 256), jnp.bfloat16),
            pltpu.VMEM((2, 2, keep, 128), jnp.bfloat16),
            pltpu.VMEM((rows, lon, n), jnp.bfloat16),
            pltpu.VMEM((units, span, lon // 2), jnp.bfloat16),
            pltpu.VMEM((units, 1, lon // 2), F32),
            pltpu.VMEM((units, blocks - 1, 1, lon // 2), F32),
            pltpu.VMEM((span, n), F32),
            pltpu.VMEM((spaces, 16, n // 2), jnp.bfloat16),
            pltpu.VMEM((spaces - 1, 16, n // 2), jnp.bfloat16),
            pltpu.VMEM((16, n // 2), jnp.bfloat16),
            pltpu.SemaphoreType.REGULAR((5,)),
            pltpu.SemaphoreType.DMA((3,)),
            pltpu.SemaphoreType.DMA,
            pltpu.SemaphoreType.DMA((2, 4)),
            pltpu.SemaphoreType.DMA((4, units)),
            pltpu.SemaphoreType.DMA((2, units)),
            pltpu.SemaphoreType.DMA((2,)),
            pltpu.SemaphoreType.DMA((4,)),
            pltpu.SemaphoreType.DMA((5 + blocks,)),
            pltpu.SemaphoreType.DMA((2, 8)),
        ],
        compiler_params=pltpu.CompilerParams(
            collective_id=0, has_side_effects=True, vmem_limit_bytes=56 * 2**20
        ),
        name="front",
    )(field, sketch, jnp.asarray(band_weights(span)), jnp.asarray(ring_weights(piece)))


def factor_block(m_ref):
    lane8 = lax.broadcasted_iota(jnp.int32, (8, 1), 0)
    for q in range(16):
        top = 8 * q
        p = m_ref[top:top + 8, :]
        cols = [jnp.broadcast_to(m_ref[top:128, top + k:top + k + 1], (128 - top, 128)) for k in range(8)]
        scaled = []
        for k in range(8):
            c = cols[k]
            d = c[k:k + 1, :]
            r = 1.0 / d
            for m in range(k + 1, 8):
                cols[m] = cols[m] - c * (cols[m][k:k + 1, :] * r)
            row = p[k:k + 1, :]
            t = row * jnp.concatenate([r, r], axis=1)
            below = jnp.where(lane8 > k, c[0:8, :], 0.0)
            p = p - jnp.concatenate([below, below], axis=1) * t
            scaled.append(t)
            s = lax.rsqrt(d)
            m_ref[top + k:top + k + 1, :] = row * jnp.concatenate([s, s], axis=1)
        if q < 15:
            left = m_ref[top + 8:128, 0:128]
            right = m_ref[top + 8:128, 128:256]
            for k in range(8):
                c = cols[k][8:, :]
                left = left - c * scaled[k][:, 0:128]
                right = right - c * scaled[k][:, 128:256]
            m_ref[top + 8:128, 0:128] = left
            m_ref[top + 8:128, 128:256] = right

def factor_kernel(root, y_ref, own_ref, basis_ref, r_ref, a_ref, m_ref, rest_ref):
    n = own_ref.shape[1]
    blocks = n // 128
    pairs = y_ref[...].astype(F32)
    y = jnp.concatenate([pairs[:, :8].reshape(-1, n // 2), pairs[:, 8:].reshape(-1, n // 2)], axis=1).astype(jnp.bfloat16)
    a_ref[...] = lax.dot_general(y, y, (((0,), (0,)), ((), ())), preferred_element_type=F32)
    rest_ref[...] = own_ref[...]
    row = lax.broadcasted_iota(jnp.int32, (128, 128), 0)
    col = lax.broadcasted_iota(jnp.int32, (128, 128), 1)

    @pl.loop(0, blocks)
    def _(b):
        here = pl.ds(pl.multiple_of(b * 128, 128), 128)
        m_ref[:, 0:128] = a_ref[here, here]
        m_ref[:, 128:256] = (row == col).astype(F32)
        factor_block(m_ref)
        inv = m_ref[:, 128:256]
        x = lax.dot_general(rest_ref[:, here], inv, (((1,), (1,)), ((), ())), precision=HI, preferred_element_type=F32)
        basis_ref[:, here] = x * root
        panel = jnp.dot(inv, a_ref[here, :], precision=HI, preferred_element_type=F32)
        wide = lax.broadcasted_iota(jnp.int32, (128, n), 1) >= (b + 1) * 128
        panel = jnp.where(wide, panel, 0.0)
        r_ref[here, :] = panel * (1.0 / root)
        r_ref[here, here] = jnp.where(row <= col, m_ref[:, 0:128], 0.0) * (1.0 / root)
        rest_ref[...] -= jnp.dot(x, panel, precision=HI, preferred_element_type=F32)
        a_ref[...] -= lax.dot_general(panel, panel, (((0,), (0,)), ((), ())), precision=HI, preferred_element_type=F32)

def factor(y, own, hours):
    n = own.shape[1]
    return pl.pallas_call(
        functools.partial(factor_kernel, math.sqrt(hours)),
        out_shape=(jax.ShapeDtypeStruct((own.shape[0], n), F32), jax.ShapeDtypeStruct((n, n), F32)),
        in_specs=[pl.BlockSpec(memory_space=pltpu.VMEM)] * 2,
        out_specs=(pl.BlockSpec(memory_space=pltpu.VMEM), pl.BlockSpec(memory_space=pltpu.VMEM)),
        scratch_shapes=[pltpu.VMEM((n, n), F32), pltpu.VMEM((128, 256), F32), pltpu.VMEM((own.shape[0], n), F32)],
        compiler_params=pltpu.CompilerParams(vmem_limit_bytes=32 * 2**20),
        name="factor",
    )(y, own)


def body(field, sketch):
    spaces, blocks = lax.axis_size("space"), lax.axis_size("tm")
    all_hours = field.shape[2] * blocks
    everyone, own = front(field, sketch, spaces, blocks)
    return factor(everyone.reshape(-1, 16, everyone.shape[4]), own, all_hours)


def solution(mesh):
    placed = (P("space", None, "tm"), P("space", None, None))
    return jax.shard_map(
        body, mesh=mesh, in_specs=placed, out_specs=(P(("tm", "space"), None), P()), check_vma=False
    )
```

```python
import functools
import math

import jax
import jax.numpy as jnp
import numpy as np
from jax import lax
from jax.experimental import pallas as pl
from jax.experimental.pallas import tpu as pltpu
from jax.sharding import PartitionSpec as P

HALO = 120
F32 = jnp.float32
HI = lax.Precision.HIGH
MESH = pl.DeviceIdType.MESH
LAG = 4


low_cutoff = 1.0 / 240.0
high_cutoff = 0.4
smooth_taps = (1.0 / 16.0, 4.0 / 16.0, 6.0 / 16.0, 4.0 / 16.0, 1.0 / 16.0)


def band_weights(span):
    m = np.arange(span + 256, dtype=np.float64)[None, :] - 128.0 - np.arange(span, dtype=np.float64)[:, None]
    value = 2.0 * high_cutoff * np.sinc(2.0 * high_cutoff * m) - 2.0 * low_cutoff * np.sinc(2.0 * low_cutoff * m)
    value = value * np.sinc(m / (HALO + 1.0))
    return np.where(np.abs(m) <= HALO, value, 0.0).astype(np.float32).astype(jnp.bfloat16)


def ring_weights(piece):
    offset = np.arange(piece + 32)[None, :] - 16 - np.arange(piece)[:, None]
    value = np.zeros(offset.shape, np.float32)
    for shift in range(-2, 3):
        value = np.where(offset == shift, smooth_taps[shift + 2], value)
    return value.astype(jnp.bfloat16)


def front_kernel(
    hours,
    field_ref,
    sketch_ref,
    band_ref,
    ring_ref,
    all_ref,
    own_ref,
    x,
    series,
    packed,
    omega,
    filtered,
    energy,
    heard,
    part,
    offered,
    arrived,
    mine_ref,
    ready,
    load_sem,
    omega_sem,
    row_sem,
    rim_sem,
    energy_sem,
    sum_sem,
    sent_sem,
    gather_sem,
    pair_sem,
):
    spaces, blocks = lax.axis_size("space"), lax.axis_size("tm")
    s, t = lax.axis_index("space"), lax.axis_index("tm")
    rows, lon, span = field_ref.shape
    piece = ring_ref.shape[0]
    reach = lon // 2
    units = 2 * rows
    last = rows + 2
    chips = spaces // 2
    core, chip = lax.rem(s, 2), s // 2

    def across(q):
        return lax.rem(s + q, spaces), t

    barrier = pltpu.get_barrier_semaphore()

    own = pltpu.make_async_copy(field_ref, x.at[2:last, 16 : lon + 16], load_sem.at[0])
    left = pltpu.make_async_copy(field_ref.at[:, lon - 16 : lon], x.at[2:last, 0:16], load_sem.at[1])
    right = pltpu.make_async_copy(field_ref.at[:, 0:16], x.at[2:last, lon + 16 : lon + 32], load_sem.at[2])
    own.start()
    left.start()
    right.start()
    load_omega = pltpu.make_async_copy(sketch_ref, omega, omega_sem)

    def tell(semaphore, radius):
        for step in (radius, spaces - radius):
            pl.semaphore_signal(semaphore, inc=1, device_id=across(step), device_id_type=MESH)

    def tell_blocks(semaphore):
        for q in range(1, blocks):
            pl.semaphore_signal(semaphore, inc=1, device_id=(s, lax.rem(t + q, blocks)), device_id_type=MESH)

    tell(barrier, 1)
    tell_blocks(barrier)

    def halo(part_of, step):
        take = slice(rows - 2, rows) if step > 0 else slice(0, 2)
        give = slice(0, 2) if step > 0 else slice(last, last + 2)
        if part_of == 0:
            wrap, inner = (lon - 16, 0), (0, reach + 16)
        else:
            wrap, inner = (0, lon + 16), (reach + 16, lon)
        sems = 2 * part_of + (0 if step > 0 else 1)
        copies = []
        for low, high, to in (
            (inner[0], inner[1], inner[0] + 16),
            (wrap[0], wrap[0] + 16, wrap[1]),
        ):
            copies.append(
                pltpu.make_async_remote_copy(
                    src_ref=field_ref.at[take, low:high],
                    dst_ref=x.at[give, to : to + high - low],
                    send_sem=row_sem.at[0, sems],
                    recv_sem=row_sem.at[1, sems],
                    device_id=(s + step, t),
                    device_id_type=MESH,
                )
            )
        return copies

    def halo_wait(part_of, step, side):
        give = slice(0, 2) if step > 0 else slice(last, last + 2)
        cut = reach + 32
        whole = x.at[give, 0:cut] if part_of == 0 else x.at[give, cut : lon + 32]
        sems = 2 * part_of + (0 if step > 0 else 1)
        pltpu.make_async_copy(whole, whole, row_sem.at[side, sems]).wait()

    def smooth(first, half):
        @pl.loop(0, reach // piece)
        def _(c):
            at = pl.multiple_of(half * reach + c * piece, 16)
            horizontal = [
                jnp.dot(ring_ref[...], x[first + r, pl.ds(at, piece + 32), :], preferred_element_type=F32)
                for r in range(6)
            ]
            for r in range(2):
                total = smooth_taps[2] * horizontal[r + 2] + smooth_taps[1] * (horizontal[r + 1] + horizontal[r + 3])
                total = total + smooth_taps[0] * (horizontal[r] + horizontal[r + 4])
                series[first + r, pl.ds(at, piece), 128 : 128 + span] = total.astype(jnp.bfloat16)

    def place(u):
        early = u < 4
        half = jnp.where(early, u // 2, (u - 4) // 4)
        row = jnp.where(early, 2 + lax.rem(u, 2), lax.rem(u, 4) + 4 - 6 * (lax.rem(u, 4) // 2))
        return row, pl.ds(pl.multiple_of(half * reach, 16), reach)

    keep = packed.shape[2]
    extra = reach - keep
    pieces = HALO // 8
    lane = lax.broadcasted_iota(jnp.int32, (extra, 128), 1)

    def within(where, start, size):
        return pl.ds(pl.multiple_of(where.start + start, 16), size)

    def pack(u):
        row, where = place(u)
        for side, low, spare in ((0, span, lane < 8), (1, 128, lane >= HALO)):
            tile = slice(low, low + 128)
            ending = series[row, within(where, keep, extra), tile].astype(F32)
            for k in range(pieces):
                at = k * extra
                same = series[row, within(where, at, extra), tile].astype(F32)
                moved = pltpu.roll(ending, HALO - 8 * k, 1)
                packed[side, lax.rem(u, 2), at : at + extra, :] = jnp.where(spare, moved, same).astype(jnp.bfloat16)
            at = pieces * extra
            packed[side, lax.rem(u, 2), at:keep, :] = series[row, within(where, at, keep - at), tile]

    def unpack(u):
        row, where = place(u)
        for low, first in ((0, 8), (span + 128, 0)):
            tile = slice(low, low + 128)
            ending = jnp.zeros((extra, 128), F32)
            for k in range(pieces):
                moved = pltpu.roll(series[row, within(where, k * extra, extra), tile].astype(F32), 8 + 8 * k, 1)
                at = first + 8 * k
                ending = jnp.where((lane >= at) & (lane < at + 8), moved, ending)
            series[row, within(where, keep, extra), tile] = ending.astype(jnp.bfloat16)

    def rims(u):
        row, where = place(u)
        before = pltpu.make_async_remote_copy(
            src_ref=packed.at[0, lax.rem(u, 2)],
            dst_ref=series.at[row, within(where, 0, keep), 0:128],
            send_sem=rim_sem.at[0, u],
            recv_sem=rim_sem.at[1, u],
            device_id=(s, t + 1),
            device_id_type=MESH,
        )
        after = pltpu.make_async_remote_copy(
            src_ref=packed.at[1, lax.rem(u, 2)],
            dst_ref=series.at[row, within(where, 0, keep), span + 128 : span + 256],
            send_sem=rim_sem.at[2, u],
            recv_sem=rim_sem.at[3, u],
            device_id=(s, t - 1),
            device_id_type=MESH,
        )
        return before, after

    def send_rims(u):
        pack(u)
        before, after = rims(u)

        @pl.when(t < blocks - 1)
        def _():
            before.start()

        @pl.when(t > 0)
        def _():
            after.start()

    def sent_rims(u):
        before, after = rims(u)

        @pl.when(t < blocks - 1)
        def _():
            before.wait_send()

        @pl.when(t > 0)
        def _():
            after.wait_send()

    def filter_unit(u):
        row, where = place(u)
        before, after = rims(u)

        @pl.when(t > 0)
        def _():
            before.wait_recv()

        @pl.when(t < blocks - 1)
        def _():
            after.wait_recv()

        unpack(u)
        value = lax.dot_general(
            band_ref[...], series[row, where, :], (((1,), (1,)), ((), ())), preferred_element_type=F32
        ).astype(jnp.bfloat16)
        filtered[u] = value
        wide = value.astype(F32)
        energy[u] = jnp.sum(wide * wide, axis=0, keepdims=True)
        for q in range(1, blocks):
            pltpu.make_async_remote_copy(
                src_ref=energy.at[u],
                dst_ref=heard.at[u, q - 1],
                send_sem=energy_sem.at[0, u],
                recv_sem=energy_sem.at[1, u],
                device_id=(s, lax.rem(t + q, blocks)),
                device_id_type=MESH,
            ).start()

    def sketch_unit(u):
        row, where = place(u)
        pltpu.make_async_copy(heard.at[u], heard.at[u], energy_sem.at[1, u]).wait()
        total = energy[u]
        for q in range(blocks - 1):
            total = total + heard[u, q]
        inverse = lax.rsqrt(total / hours + 1e-06)
        standard = (filtered[u].astype(F32) * inverse).astype(jnp.bfloat16)
        part[...] += jnp.dot(standard, omega[row, where, :], preferred_element_type=F32)

    own.wait()
    left.wait()
    right.wait()
    smooth(2, 0)
    pl.semaphore_wait(barrier, blocks + 1)

    for part_of in range(2):
        for step in (1, -1):
            copies = halo(part_of, step)

            @pl.when((s < spaces - 1) if step > 0 else (s > 0))
            def _():
                for copy in copies:
                    copy.start()

    @pl.loop(0, 2)
    def _(u):
        send_rims(u)

    smooth(2, 1)
    load_omega.start()

    @pl.when(s == spaces - 1)
    def _():
        x[last : last + 2] = jnp.zeros((2, lon + 32, span), jnp.bfloat16)

    @pl.when(s == 0)
    def _():
        x[0:2] = jnp.zeros((2, lon + 32, span), jnp.bfloat16)

    @pl.when(t == 0)
    def _():
        series[:, :, 0:128] = jnp.zeros((rows, lon, 128), jnp.bfloat16)

    @pl.when(t == blocks - 1)
    def _():
        series[:, :, span + 128 : span + 256] = jnp.zeros((rows, lon, 128), jnp.bfloat16)

    part[...] = jnp.zeros(part.shape, F32)
    load_omega.wait()

    @pl.loop(2, units + LAG)
    def _(n):
        for part_of in range(2):

            @pl.when(n == 4 + 4 * part_of)
            def _():
                @pl.when(s < spaces - 1)
                def _():
                    halo_wait(part_of, -1, 1)

                @pl.when(s > 0)
                def _():
                    halo_wait(part_of, 1, 1)

        @pl.when((n == 4) | (n == 8))
        def _():
            @pl.loop(0, 2)
            def _(k):
                smooth(4 - 4 * k, (n - 4) // 4)

        @pl.when(n < units)
        def _():
            sent_rims(n - 2)
            send_rims(n)

        for k in range(5):

            @pl.when(n == 5 + k)
            def _():
                if k:
                    pl.semaphore_wait(ready.at[k - 1], 2)
                if k < 4:
                    tell(ready.at[k], 2**k)
                else:
                    tell_blocks(ready.at[k])

        @pl.when(n < units + 2)
        def _():
            filter_unit(n - 2)

        @pl.when(n >= LAG)
        def _():
            sketch_unit(n - LAG)

    pl.semaphore_wait(ready.at[4], blocks - 1)
    half = part.shape[1] // 2
    split = part[...].reshape(spaces, span // spaces, 2 * half)
    offered[...] = jnp.concatenate([split[:, :, :half], split[:, :, half:]], axis=1).astype(jnp.bfloat16)

    @pl.loop(1, spaces)
    def _(q):
        to, _ = across(q)
        pltpu.make_async_remote_copy(
            src_ref=offered.at[to],
            dst_ref=arrived.at[q - 1],
            send_sem=sum_sem.at[0],
            recv_sem=sum_sem.at[1],
            device_id=across(q),
            device_id_type=MESH,
        ).start()

    near = part[pl.ds(pl.multiple_of(s * 8, 8), 8), :]
    pltpu.make_async_copy(arrived, arrived, sum_sem.at[1]).wait()
    total = jnp.concatenate([near[:, :half], near[:, half:]], axis=0)
    for q in range(spaces - 1):
        total = total + arrived[q].astype(F32)
    own_ref[:, :half] = total[:8]
    own_ref[:, half:] = total[8:]
    mine_ref[...] = total.astype(jnp.bfloat16)
    all_ref[core, t, chip] = total.astype(jnp.bfloat16)
    first, second = slice(0, half // 2), slice(half // 2, half)
    near_chips = chips // 4

    def block_peer(q):
        return s, lax.rem(t + q, blocks)

    def chip_peer(c):
        return 2 * lax.rem(chip + c, chips) + core, t

    def give(ref, to, kind, recv_sem, peer):
        pltpu.make_async_remote_copy(
            src_ref=ref,
            dst_ref=to,
            send_sem=sent_sem.at[kind],
            recv_sem=recv_sem,
            device_id=peer,
            device_id_type=MESH,
        ).start()

    def settle(ref, semaphore):
        pltpu.make_async_copy(ref, ref, semaphore).wait()

    for q in range(1, blocks):
        give(mine_ref.at[:, first], all_ref.at[core, t, chip, :, first], 0, gather_sem.at[0], block_peer(q))

    @pl.loop(1, chips)
    def _(c):
        give(mine_ref.at[:, second], all_ref.at[core, t, chip, :, second], 1, gather_sem.at[1], chip_peer(c))

    settle(all_ref.at[core, pl.ds(0, blocks - 1), chip, :, first], gather_sem.at[0])
    column = all_ref.at[core, :, chip, :, first]

    @pl.loop(1, chips)
    def _(c):
        give(column, column, 2, gather_sem.at[2 + chip // near_chips], chip_peer(c))

    settle(all_ref.at[core, t, pl.ds(0, chips - 1), :, second], gather_sem.at[1])
    plane = all_ref.at[core, t, :, :, second]
    for q in range(1, blocks):
        give(plane, plane, 3, gather_sem.at[5 + q], block_peer(q))

    def pair(k):
        j = k // 2
        if k % 2:
            group = all_ref.at[core, lax.rem(t + blocks - (0, 1, 3, 2)[j], blocks), :, :, second]
        else:
            at = lax.rem(chip // near_chips + j, 4) * near_chips
            group = all_ref.at[core, :, pl.ds(at, near_chips), :, first]
        return pltpu.make_async_remote_copy(
            src_ref=group,
            dst_ref=group,
            send_sem=pair_sem.at[0, k],
            recv_sem=pair_sem.at[1, k],
            device_id=(2 * chip + 1 - core, t),
            device_id_type=MESH,
        )

    for k in (1, 0, 3, 2, 5, 4, 7, 6):
        j = k // 2
        if k % 2:
            if j:
                settle(plane, gather_sem.at[5 + (0, 1, 3, 2)[j]])
        else:
            count = near_chips - 1 if j == 0 else near_chips
            settle(
                all_ref.at[core, :, pl.ds(0, count), :, first],
                gather_sem.at[2 + lax.rem(chip // near_chips + j, 4)],
            )
        pair(k).start()

    for part_of in range(2):
        for step in (1, -1):

            @pl.when((s < spaces - 1) if step > 0 else (s > 0))
            def _():
                halo_wait(part_of, step, 0)

    sent_rims(units - 2)
    sent_rims(units - 1)

    @pl.loop(0, units)
    def _(u):
        pltpu.make_async_copy(heard.at[u], heard.at[u], energy_sem.at[0, u]).wait()

    pltpu.make_async_copy(arrived, arrived, sum_sem.at[0]).wait()
    settle(all_ref.at[core, pl.ds(0, blocks - 1), chip, :, first], sent_sem.at[0])
    settle(all_ref.at[core, t, pl.ds(0, chips - 1), :, second], sent_sem.at[1])
    settle(all_ref.at[core, :, pl.ds(0, chips - 1), :, first], sent_sem.at[2])
    settle(all_ref.at[core, pl.ds(0, blocks - 1), :, :, second], sent_sem.at[3])
    for k in range(8):
        pair(k).wait()


def front(field, sketch, spaces, blocks):
    rows, lon, span = field.shape
    n = sketch.shape[2]
    piece, chips, units = 144, spaces // 2, 2 * rows
    keep = -(-lon * HALO // 4096) * 16
    vmem = pl.BlockSpec(memory_space=pltpu.VMEM)
    hbm = pl.BlockSpec(memory_space=pl.ANY)
    return pl.pallas_call(
        functools.partial(front_kernel, span * blocks),
        out_shape=(
            jax.ShapeDtypeStruct((2, blocks, chips, 16, n // 2), jnp.bfloat16),
            jax.ShapeDtypeStruct((8, n), F32),
        ),
        in_specs=[hbm, hbm, vmem, vmem],
        out_specs=(vmem, vmem),
        scratch_shapes=[
            pltpu.VMEM((rows + 4, lon + 32, span), jnp.bfloat16),
            pltpu.VMEM((rows, lon, span + 256), jnp.bfloat16),
            pltpu.VMEM((2, 2, keep, 128), jnp.bfloat16),
            pltpu.VMEM((rows, lon, n), jnp.bfloat16),
            pltpu.VMEM((units, span, lon // 2), jnp.bfloat16),
            pltpu.VMEM((units, 1, lon // 2), F32),
            pltpu.VMEM((units, blocks - 1, 1, lon // 2), F32),
            pltpu.VMEM((span, n), F32),
            pltpu.VMEM((spaces, 16, n // 2), jnp.bfloat16),
            pltpu.VMEM((spaces - 1, 16, n // 2), jnp.bfloat16),
            pltpu.VMEM((16, n // 2), jnp.bfloat16),
            pltpu.SemaphoreType.REGULAR((5,)),
            pltpu.SemaphoreType.DMA((3,)),
            pltpu.SemaphoreType.DMA,
            pltpu.SemaphoreType.DMA((2, 4)),
            pltpu.SemaphoreType.DMA((4, units)),
            pltpu.SemaphoreType.DMA((2, units)),
            pltpu.SemaphoreType.DMA((2,)),
            pltpu.SemaphoreType.DMA((4,)),
            pltpu.SemaphoreType.DMA((5 + blocks,)),
            pltpu.SemaphoreType.DMA((2, 8)),
        ],
        compiler_params=pltpu.CompilerParams(
            collective_id=0, has_side_effects=True, vmem_limit_bytes=56 * 2**20
        ),
        name="front",
    )(field, sketch, jnp.asarray(band_weights(span)), jnp.asarray(ring_weights(piece)))


def factor_block(m_ref):
    lane8 = lax.broadcasted_iota(jnp.int32, (8, 1), 0)
    for q in range(16):
        top = 8 * q
        p = m_ref[top:top + 8, :]
        cols = [jnp.broadcast_to(m_ref[top:128, top + k:top + k + 1], (128 - top, 128)) for k in range(8)]
        scaled = []
        for k in range(8):
            c = cols[k]
            d = c[k:k + 1, :]
            r = 1.0 / d
            for m in range(k + 1, 8):
                cols[m] = cols[m] - c * (cols[m][k:k + 1, :] * r)
            row = p[k:k + 1, :]
            t = row * jnp.concatenate([r, r], axis=1)
            below = jnp.where(lane8 > k, c[0:8, :], 0.0)
            p = p - jnp.concatenate([below, below], axis=1) * t
            scaled.append(t)
            s = lax.rsqrt(d)
            m_ref[top + k:top + k + 1, :] = row * jnp.concatenate([s, s], axis=1)
        if q < 15:
            left = m_ref[top + 8:128, 0:128]
            right = m_ref[top + 8:128, 128:256]
            for k in range(8):
                c = cols[k][8:, :]
                left = left - c * scaled[k][:, 0:128]
                right = right - c * scaled[k][:, 128:256]
            m_ref[top + 8:128, 0:128] = left
            m_ref[top + 8:128, 128:256] = right

def factor_kernel(root, y_ref, own_ref, basis_ref, r_ref, a_ref, m_ref, rest_ref):
    n = own_ref.shape[1]
    blocks = n // 128
    pairs = y_ref[...].astype(F32)
    y = jnp.concatenate([pairs[:, :8].reshape(-1, n // 2), pairs[:, 8:].reshape(-1, n // 2)], axis=1).astype(jnp.bfloat16)
    a_ref[...] = lax.dot_general(y, y, (((0,), (0,)), ((), ())), preferred_element_type=F32)
    rest_ref[...] = own_ref[...]
    row = lax.broadcasted_iota(jnp.int32, (128, 128), 0)
    col = lax.broadcasted_iota(jnp.int32, (128, 128), 1)

    @pl.loop(0, blocks)
    def _(b):
        here = pl.ds(pl.multiple_of(b * 128, 128), 128)
        m_ref[:, 0:128] = a_ref[here, here]
        m_ref[:, 128:256] = (row == col).astype(F32)
        factor_block(m_ref)
        inv = m_ref[:, 128:256]
        x = lax.dot_general(rest_ref[:, here], inv, (((1,), (1,)), ((), ())), precision=HI, preferred_element_type=F32)
        basis_ref[:, here] = x * root
        panel = jnp.dot(inv, a_ref[here, :], precision=HI, preferred_element_type=F32)
        wide = lax.broadcasted_iota(jnp.int32, (128, n), 1) >= (b + 1) * 128
        panel = jnp.where(wide, panel, 0.0)
        r_ref[here, :] = panel * (1.0 / root)
        r_ref[here, here] = jnp.where(row <= col, m_ref[:, 0:128], 0.0) * (1.0 / root)
        rest_ref[...] -= jnp.dot(x, panel, precision=HI, preferred_element_type=F32)
        a_ref[...] -= lax.dot_general(panel, panel, (((0,), (0,)), ((), ())), precision=HI, preferred_element_type=F32)

def factor(y, own, hours):
    n = own.shape[1]
    return pl.pallas_call(
        functools.partial(factor_kernel, math.sqrt(hours)),
        out_shape=(jax.ShapeDtypeStruct((own.shape[0], n), F32), jax.ShapeDtypeStruct((n, n), F32)),
        in_specs=[pl.BlockSpec(memory_space=pltpu.VMEM)] * 2,
        out_specs=(pl.BlockSpec(memory_space=pltpu.VMEM), pl.BlockSpec(memory_space=pltpu.VMEM)),
        scratch_shapes=[pltpu.VMEM((n, n), F32), pltpu.VMEM((128, 256), F32), pltpu.VMEM((own.shape[0], n), F32)],
        compiler_params=pltpu.CompilerParams(vmem_limit_bytes=62 * 2**20),
        name="factor",
    )(y, own)


def body(field, sketch):
    spaces, blocks = lax.axis_size("space"), lax.axis_size("tm")
    all_hours = field.shape[2] * blocks
    everyone, own = front(field, sketch, spaces, blocks)
    return factor(everyone.reshape(-1, 16, everyone.shape[4]), own, all_hours)


def solution(mesh):
    placed = (P("space", None, "tm"), P("space", None, None))
    return jax.shard_map(
        body, mesh=mesh, in_specs=placed, out_specs=(P(("tm", "space"), None), P()), check_vma=False
    )
```

```python
import functools
import math

import jax
import jax.numpy as jnp
import numpy as np
from jax import lax
from jax.experimental import pallas as pl
from jax.experimental.pallas import tpu as pltpu
from jax.sharding import PartitionSpec as P

HALO = 120
F32 = jnp.float32
HI = lax.Precision.HIGH
MESH = pl.DeviceIdType.MESH
LAG = 5


low_cutoff = 1.0 / 240.0
high_cutoff = 0.4
smooth_taps = (1.0 / 16.0, 4.0 / 16.0, 6.0 / 16.0, 4.0 / 16.0, 1.0 / 16.0)


def band_weights(span):
    m = np.arange(span + 256, dtype=np.float64)[None, :] - 128.0 - np.arange(span, dtype=np.float64)[:, None]
    value = 2.0 * high_cutoff * np.sinc(2.0 * high_cutoff * m) - 2.0 * low_cutoff * np.sinc(2.0 * low_cutoff * m)
    value = value * np.sinc(m / (HALO + 1.0))
    return np.where(np.abs(m) <= HALO, value, 0.0).astype(np.float32).astype(jnp.bfloat16)


def ring_weights(piece):
    offset = np.arange(piece + 32)[None, :] - 16 - np.arange(piece)[:, None]
    value = np.zeros(offset.shape, np.float32)
    for shift in range(-2, 3):
        value = np.where(offset == shift, smooth_taps[shift + 2], value)
    return value.astype(jnp.bfloat16)


def front_kernel(
    hours,
    field_ref,
    sketch_ref,
    band_ref,
    ring_ref,
    all_ref,
    own_ref,
    x,
    series,
    packed,
    omega,
    filtered,
    energy,
    heard,
    part,
    offered,
    arrived,
    mine_ref,
    ready,
    load_sem,
    omega_sem,
    row_sem,
    rim_sem,
    energy_sem,
    sum_sem,
    sent_sem,
    gather_sem,
    pair_sem,
):
    spaces, blocks = lax.axis_size("space"), lax.axis_size("tm")
    s, t = lax.axis_index("space"), lax.axis_index("tm")
    rows, lon, span = field_ref.shape
    piece = ring_ref.shape[0]
    reach = lon // 2
    units = 2 * rows
    last = rows + 2
    chips = spaces // 2
    core, chip = lax.rem(s, 2), s // 2

    def across(q):
        return lax.rem(s + q, spaces), t

    barrier = pltpu.get_barrier_semaphore()

    own = pltpu.make_async_copy(field_ref, x.at[2:last, 16 : lon + 16], load_sem.at[0])
    left = pltpu.make_async_copy(field_ref.at[:, lon - 16 : lon], x.at[2:last, 0:16], load_sem.at[1])
    right = pltpu.make_async_copy(field_ref.at[:, 0:16], x.at[2:last, lon + 16 : lon + 32], load_sem.at[2])
    own.start()
    left.start()
    right.start()
    load_omega = pltpu.make_async_copy(sketch_ref, omega, omega_sem)

    def tell(semaphore, radius):
        for step in (radius, spaces - radius):
            pl.semaphore_signal(semaphore, inc=1, device_id=across(step), device_id_type=MESH)

    def tell_blocks(semaphore):
        for q in range(1, blocks):
            pl.semaphore_signal(semaphore, inc=1, device_id=(s, lax.rem(t + q, blocks)), device_id_type=MESH)

    tell(barrier, 1)
    tell_blocks(barrier)

    def halo(part_of, step):
        take = slice(rows - 2, rows) if step > 0 else slice(0, 2)
        give = slice(0, 2) if step > 0 else slice(last, last + 2)
        if part_of == 0:
            wrap, inner = (lon - 16, 0), (0, reach + 16)
        else:
            wrap, inner = (0, lon + 16), (reach + 16, lon)
        sems = 2 * part_of + (0 if step > 0 else 1)
        copies = []
        for low, high, to in (
            (inner[0], inner[1], inner[0] + 16),
            (wrap[0], wrap[0] + 16, wrap[1]),
        ):
            copies.append(
                pltpu.make_async_remote_copy(
                    src_ref=field_ref.at[take, low:high],
                    dst_ref=x.at[give, to : to + high - low],
                    send_sem=row_sem.at[0, sems],
                    recv_sem=row_sem.at[1, sems],
                    device_id=(s + step, t),
                    device_id_type=MESH,
                )
            )
        return copies

    def halo_wait(part_of, step, side):
        give = slice(0, 2) if step > 0 else slice(last, last + 2)
        cut = reach + 32
        whole = x.at[give, 0:cut] if part_of == 0 else x.at[give, cut : lon + 32]
        sems = 2 * part_of + (0 if step > 0 else 1)
        pltpu.make_async_copy(whole, whole, row_sem.at[side, sems]).wait()

    def smooth(first, half):
        @pl.loop(0, reach // piece)
        def _(c):
            at = pl.multiple_of(half * reach + c * piece, 16)
            horizontal = [
                jnp.dot(ring_ref[...], x[first + r, pl.ds(at, piece + 32), :], preferred_element_type=F32)
                for r in range(6)
            ]
            for r in range(2):
                total = smooth_taps[2] * horizontal[r + 2] + smooth_taps[1] * (horizontal[r + 1] + horizontal[r + 3])
                total = total + smooth_taps[0] * (horizontal[r] + horizontal[r + 4])
                series[first + r, pl.ds(at, piece), 128 : 128 + span] = total.astype(jnp.bfloat16)

    def place(u):
        early = u < 4
        half = jnp.where(early, u // 2, (u - 4) // 4)
        row = jnp.where(early, 2 + lax.rem(u, 2), lax.rem(u, 4) + 4 - 6 * (lax.rem(u, 4) // 2))
        return row, pl.ds(pl.multiple_of(half * reach, 16), reach)

    keep = packed.shape[2]
    extra = reach - keep
    pieces = HALO // 8
    lane = lax.broadcasted_iota(jnp.int32, (extra, 128), 1)

    def within(where, start, size):
        return pl.ds(pl.multiple_of(where.start + start, 16), size)

    def pack(u):
        row, where = place(u)
        for side, low, spare in ((0, span, lane < 8), (1, 128, lane >= HALO)):
            tile = slice(low, low + 128)
            ending = series[row, within(where, keep, extra), tile].astype(F32)
            for k in range(pieces):
                at = k * extra
                same = series[row, within(where, at, extra), tile].astype(F32)
                moved = pltpu.roll(ending, HALO - 8 * k, 1)
                packed[side, lax.rem(u, 2), at : at + extra, :] = jnp.where(spare, moved, same).astype(jnp.bfloat16)
            at = pieces * extra
            packed[side, lax.rem(u, 2), at:keep, :] = series[row, within(where, at, keep - at), tile]

    def unpack(u):
        row, where = place(u)
        for low, first in ((0, 8), (span + 128, 0)):
            tile = slice(low, low + 128)
            ending = jnp.zeros((extra, 128), F32)
            for k in range(pieces):
                moved = pltpu.roll(series[row, within(where, k * extra, extra), tile].astype(F32), 8 + 8 * k, 1)
                at = first + 8 * k
                ending = jnp.where((lane >= at) & (lane < at + 8), moved, ending)
            series[row, within(where, keep, extra), tile] = ending.astype(jnp.bfloat16)

    def rims(u):
        row, where = place(u)
        before = pltpu.make_async_remote_copy(
            src_ref=packed.at[0, lax.rem(u, 2)],
            dst_ref=series.at[row, within(where, 0, keep), 0:128],
            send_sem=rim_sem.at[0, u],
            recv_sem=rim_sem.at[1, u],
            device_id=(s, t + 1),
            device_id_type=MESH,
        )
        after = pltpu.make_async_remote_copy(
            src_ref=packed.at[1, lax.rem(u, 2)],
            dst_ref=series.at[row, within(where, 0, keep), span + 128 : span + 256],
            send_sem=rim_sem.at[2, u],
            recv_sem=rim_sem.at[3, u],
            device_id=(s, t - 1),
            device_id_type=MESH,
        )
        return before, after

    def send_rims(u):
        pack(u)
        before, after = rims(u)

        @pl.when(t < blocks - 1)
        def _():
            before.start()

        @pl.when(t > 0)
        def _():
            after.start()

    def sent_rims(u):
        before, after = rims(u)

        @pl.when(t < blocks - 1)
        def _():
            before.wait_send()

        @pl.when(t > 0)
        def _():
            after.wait_send()

    def filter_unit(u):
        row, where = place(u)
        before, after = rims(u)

        @pl.when(t > 0)
        def _():
            before.wait_recv()

        @pl.when(t < blocks - 1)
        def _():
            after.wait_recv()

        unpack(u)
        value = lax.dot_general(
            band_ref[...], series[row, where, :], (((1,), (1,)), ((), ())), preferred_element_type=F32
        ).astype(jnp.bfloat16)
        filtered[u] = value
        wide = value.astype(F32)
        energy[u] = jnp.sum(wide * wide, axis=0, keepdims=True)
        for q in range(1, blocks):
            pltpu.make_async_remote_copy(
                src_ref=energy.at[u],
                dst_ref=heard.at[u, q - 1],
                send_sem=energy_sem.at[0, u],
                recv_sem=energy_sem.at[1, u],
                device_id=(s, lax.rem(t + q, blocks)),
                device_id_type=MESH,
            ).start()

    def sketch_unit(u):
        row, where = place(u)
        pltpu.make_async_copy(heard.at[u], heard.at[u], energy_sem.at[1, u]).wait()
        total = energy[u]
        for q in range(blocks - 1):
            total = total + heard[u, q]
        inverse = lax.rsqrt(total / hours + 1e-06)
        standard = (filtered[u].astype(F32) * inverse).astype(jnp.bfloat16)
        part[...] += jnp.dot(standard, omega[row, where, :], preferred_element_type=F32)

    own.wait()
    left.wait()
    right.wait()
    smooth(2, 0)
    pl.semaphore_wait(barrier, blocks + 1)

    for part_of in range(2):
        for step in (1, -1):
            copies = halo(part_of, step)

            @pl.when((s < spaces - 1) if step > 0 else (s > 0))
            def _():
                for copy in copies:
                    copy.start()

    @pl.loop(0, 2)
    def _(u):
        send_rims(u)

    smooth(2, 1)
    load_omega.start()

    @pl.when(s == spaces - 1)
    def _():
        x[last : last + 2] = jnp.zeros((2, lon + 32, span), jnp.bfloat16)

    @pl.when(s == 0)
    def _():
        x[0:2] = jnp.zeros((2, lon + 32, span), jnp.bfloat16)

    @pl.when(t == 0)
    def _():
        series[:, :, 0:128] = jnp.zeros((rows, lon, 128), jnp.bfloat16)

    @pl.when(t == blocks - 1)
    def _():
        series[:, :, span + 128 : span + 256] = jnp.zeros((rows, lon, 128), jnp.bfloat16)

    part[...] = jnp.zeros(part.shape, F32)
    load_omega.wait()

    @pl.loop(2, units + LAG)
    def _(n):
        for part_of in range(2):

            @pl.when(n == 4 + 4 * part_of)
            def _():
                @pl.when(s < spaces - 1)
                def _():
                    halo_wait(part_of, -1, 1)

                @pl.when(s > 0)
                def _():
                    halo_wait(part_of, 1, 1)

        @pl.when((n == 4) | (n == 8))
        def _():
            @pl.loop(0, 2)
            def _(k):
                smooth(4 - 4 * k, (n - 4) // 4)

        @pl.when(n < units)
        def _():
            sent_rims(n - 2)
            send_rims(n)

        for k in range(5):

            @pl.when(n == 5 + k)
            def _():
                if k:
                    pl.semaphore_wait(ready.at[k - 1], 2)
                if k < 4:
                    tell(ready.at[k], 2**k)
                else:
                    tell_blocks(ready.at[k])

        @pl.when(n < units + 2)
        def _():
            filter_unit(n - 2)

        @pl.when(n >= LAG)
        def _():
            sketch_unit(n - LAG)

    pl.semaphore_wait(ready.at[4], blocks - 1)
    half = part.shape[1] // 2
    split = part[...].reshape(spaces, span // spaces, 2 * half)
    offered[...] = jnp.concatenate([split[:, :, :half], split[:, :, half:]], axis=1).astype(jnp.bfloat16)

    @pl.loop(1, spaces)
    def _(q):
        to, _ = across(q)
        pltpu.make_async_remote_copy(
            src_ref=offered.at[to],
            dst_ref=arrived.at[q - 1],
            send_sem=sum_sem.at[0],
            recv_sem=sum_sem.at[1],
            device_id=across(q),
            device_id_type=MESH,
        ).start()

    near = part[pl.ds(pl.multiple_of(s * 8, 8), 8), :]
    pltpu.make_async_copy(arrived, arrived, sum_sem.at[1]).wait()
    total = jnp.concatenate([near[:, :half], near[:, half:]], axis=0)
    for q in range(spaces - 1):
        total = total + arrived[q].astype(F32)
    own_ref[:, :half] = total[:8]
    own_ref[:, half:] = total[8:]
    mine_ref[...] = total.astype(jnp.bfloat16)
    all_ref[core, t, chip] = total.astype(jnp.bfloat16)
    first, second = slice(0, half // 2), slice(half // 2, half)
    near_chips = chips // 4

    def block_peer(q):
        return s, lax.rem(t + q, blocks)

    def chip_peer(c):
        return 2 * lax.rem(chip + c, chips) + core, t

    def give(ref, to, kind, recv_sem, peer):
        pltpu.make_async_remote_copy(
            src_ref=ref,
            dst_ref=to,
            send_sem=sent_sem.at[kind],
            recv_sem=recv_sem,
            device_id=peer,
            device_id_type=MESH,
        ).start()

    def settle(ref, semaphore):
        pltpu.make_async_copy(ref, ref, semaphore).wait()

    for q in range(1, blocks):
        give(mine_ref.at[:, first], all_ref.at[core, t, chip, :, first], 0, gather_sem.at[0], block_peer(q))

    @pl.loop(1, chips)
    def _(c):
        give(mine_ref.at[:, second], all_ref.at[core, t, chip, :, second], 1, gather_sem.at[1], chip_peer(c))

    settle(all_ref.at[core, pl.ds(0, blocks - 1), chip, :, first], gather_sem.at[0])
    column = all_ref.at[core, :, chip, :, first]

    @pl.loop(1, chips)
    def _(c):
        give(column, column, 2, gather_sem.at[2 + chip // near_chips], chip_peer(c))

    settle(all_ref.at[core, t, pl.ds(0, chips - 1), :, second], gather_sem.at[1])
    plane = all_ref.at[core, t, :, :, second]
    for q in range(1, blocks):
        give(plane, plane, 3, gather_sem.at[5 + q], block_peer(q))

    def pair(k):
        j = k // 2
        if k % 2:
            group = all_ref.at[core, lax.rem(t + blocks - (0, 1, 3, 2)[j], blocks), :, :, second]
        else:
            at = lax.rem(chip // near_chips + j, 4) * near_chips
            group = all_ref.at[core, :, pl.ds(at, near_chips), :, first]
        return pltpu.make_async_remote_copy(
            src_ref=group,
            dst_ref=group,
            send_sem=pair_sem.at[0, k],
            recv_sem=pair_sem.at[1, k],
            device_id=(2 * chip + 1 - core, t),
            device_id_type=MESH,
        )

    for k in (1, 0, 3, 2, 5, 4, 7, 6):
        j = k // 2
        if k % 2:
            if j:
                settle(plane, gather_sem.at[5 + (0, 1, 3, 2)[j]])
        else:
            count = near_chips - 1 if j == 0 else near_chips
            settle(
                all_ref.at[core, :, pl.ds(0, count), :, first],
                gather_sem.at[2 + lax.rem(chip // near_chips + j, 4)],
            )
        pair(k).start()

    for part_of in range(2):
        for step in (1, -1):

            @pl.when((s < spaces - 1) if step > 0 else (s > 0))
            def _():
                halo_wait(part_of, step, 0)

    sent_rims(units - 2)
    sent_rims(units - 1)

    @pl.loop(0, units)
    def _(u):
        pltpu.make_async_copy(heard.at[u], heard.at[u], energy_sem.at[0, u]).wait()

    pltpu.make_async_copy(arrived, arrived, sum_sem.at[0]).wait()
    settle(all_ref.at[core, pl.ds(0, blocks - 1), chip, :, first], sent_sem.at[0])
    settle(all_ref.at[core, t, pl.ds(0, chips - 1), :, second], sent_sem.at[1])
    settle(all_ref.at[core, :, pl.ds(0, chips - 1), :, first], sent_sem.at[2])
    settle(all_ref.at[core, pl.ds(0, blocks - 1), :, :, second], sent_sem.at[3])
    for k in range(8):
        pair(k).wait()


def front(field, sketch, spaces, blocks):
    rows, lon, span = field.shape
    n = sketch.shape[2]
    piece, chips, units = 144, spaces // 2, 2 * rows
    keep = -(-lon * HALO // 4096) * 16
    vmem = pl.BlockSpec(memory_space=pltpu.VMEM)
    hbm = pl.BlockSpec(memory_space=pl.ANY)
    return pl.pallas_call(
        functools.partial(front_kernel, span * blocks),
        out_shape=(
            jax.ShapeDtypeStruct((2, blocks, chips, 16, n // 2), jnp.bfloat16),
            jax.ShapeDtypeStruct((8, n), F32),
        ),
        in_specs=[hbm, hbm, vmem, vmem],
        out_specs=(vmem, vmem),
        scratch_shapes=[
            pltpu.VMEM((rows + 4, lon + 32, span), jnp.bfloat16),
            pltpu.VMEM((rows, lon, span + 256), jnp.bfloat16),
            pltpu.VMEM((2, 2, keep, 128), jnp.bfloat16),
            pltpu.VMEM((rows, lon, n), jnp.bfloat16),
            pltpu.VMEM((units, span, lon // 2), jnp.bfloat16),
            pltpu.VMEM((units, 1, lon // 2), F32),
            pltpu.VMEM((units, blocks - 1, 1, lon // 2), F32),
            pltpu.VMEM((span, n), F32),
            pltpu.VMEM((spaces, 16, n // 2), jnp.bfloat16),
            pltpu.VMEM((spaces - 1, 16, n // 2), jnp.bfloat16),
            pltpu.VMEM((16, n // 2), jnp.bfloat16),
            pltpu.SemaphoreType.REGULAR((5,)),
            pltpu.SemaphoreType.DMA((3,)),
            pltpu.SemaphoreType.DMA,
            pltpu.SemaphoreType.DMA((2, 4)),
            pltpu.SemaphoreType.DMA((4, units)),
            pltpu.SemaphoreType.DMA((2, units)),
            pltpu.SemaphoreType.DMA((2,)),
            pltpu.SemaphoreType.DMA((4,)),
            pltpu.SemaphoreType.DMA((5 + blocks,)),
            pltpu.SemaphoreType.DMA((2, 8)),
        ],
        compiler_params=pltpu.CompilerParams(
            collective_id=0, has_side_effects=True, vmem_limit_bytes=56 * 2**20
        ),
        name="front",
    )(field, sketch, jnp.asarray(band_weights(span)), jnp.asarray(ring_weights(piece)))


def factor_block(m_ref):
    lane8 = lax.broadcasted_iota(jnp.int32, (8, 1), 0)
    for q in range(16):
        top = 8 * q
        p = m_ref[top:top + 8, :]
        cols = [jnp.broadcast_to(m_ref[top:128, top + k:top + k + 1], (128 - top, 128)) for k in range(8)]
        scaled = []
        for k in range(8):
            c = cols[k]
            d = c[k:k + 1, :]
            r = 1.0 / d
            for m in range(k + 1, 8):
                cols[m] = cols[m] - c * (cols[m][k:k + 1, :] * r)
            row = p[k:k + 1, :]
            t = row * jnp.concatenate([r, r], axis=1)
            below = jnp.where(lane8 > k, c[0:8, :], 0.0)
            p = p - jnp.concatenate([below, below], axis=1) * t
            scaled.append(t)
            s = lax.rsqrt(d)
            m_ref[top + k:top + k + 1, :] = row * jnp.concatenate([s, s], axis=1)
        if q < 15:
            left = m_ref[top + 8:128, 0:128]
            right = m_ref[top + 8:128, 128:256]
            for k in range(8):
                c = cols[k][8:, :]
                left = left - c * scaled[k][:, 0:128]
                right = right - c * scaled[k][:, 128:256]
            m_ref[top + 8:128, 0:128] = left
            m_ref[top + 8:128, 128:256] = right

def factor_kernel(root, y_ref, own_ref, basis_ref, r_ref, a_ref, m_ref, rest_ref):
    n = own_ref.shape[1]
    blocks = n // 128
    pairs = y_ref[...].astype(F32)
    y = jnp.concatenate([pairs[:, :8].reshape(-1, n // 2), pairs[:, 8:].reshape(-1, n // 2)], axis=1).astype(jnp.bfloat16)
    a_ref[...] = lax.dot_general(y, y, (((0,), (0,)), ((), ())), preferred_element_type=F32)
    rest_ref[...] = own_ref[...]
    row = lax.broadcasted_iota(jnp.int32, (128, 128), 0)
    col = lax.broadcasted_iota(jnp.int32, (128, 128), 1)

    @pl.loop(0, blocks)
    def _(b):
        here = pl.ds(pl.multiple_of(b * 128, 128), 128)
        m_ref[:, 0:128] = a_ref[here, here]
        m_ref[:, 128:256] = (row == col).astype(F32)
        factor_block(m_ref)
        inv = m_ref[:, 128:256]
        x = lax.dot_general(rest_ref[:, here], inv, (((1,), (1,)), ((), ())), precision=HI, preferred_element_type=F32)
        basis_ref[:, here] = x * root
        panel = jnp.dot(inv, a_ref[here, :], precision=HI, preferred_element_type=F32)
        wide = lax.broadcasted_iota(jnp.int32, (128, n), 1) >= (b + 1) * 128
        panel = jnp.where(wide, panel, 0.0)
        r_ref[here, :] = panel * (1.0 / root)
        r_ref[here, here] = jnp.where(row <= col, m_ref[:, 0:128], 0.0) * (1.0 / root)
        rest_ref[...] -= jnp.dot(x, panel, precision=HI, preferred_element_type=F32)
        a_ref[...] -= lax.dot_general(panel, panel, (((0,), (0,)), ((), ())), precision=HI, preferred_element_type=F32)

def factor(y, own, hours):
    n = own.shape[1]
    return pl.pallas_call(
        functools.partial(factor_kernel, math.sqrt(hours)),
        out_shape=(jax.ShapeDtypeStruct((own.shape[0], n), F32), jax.ShapeDtypeStruct((n, n), F32)),
        in_specs=[pl.BlockSpec(memory_space=pltpu.VMEM)] * 2,
        out_specs=(pl.BlockSpec(memory_space=pltpu.VMEM), pl.BlockSpec(memory_space=pltpu.VMEM)),
        scratch_shapes=[pltpu.VMEM((n, n), F32), pltpu.VMEM((128, 256), F32), pltpu.VMEM((own.shape[0], n), F32)],
        compiler_params=pltpu.CompilerParams(vmem_limit_bytes=62 * 2**20),
        name="factor",
    )(y, own)


def body(field, sketch):
    spaces, blocks = lax.axis_size("space"), lax.axis_size("tm")
    all_hours = field.shape[2] * blocks
    everyone, own = front(field, sketch, spaces, blocks)
    return factor(everyone.reshape(-1, 16, everyone.shape[4]), own, all_hours)


def solution(mesh):
    placed = (P("space", None, "tm"), P("space", None, None))
    return jax.shard_map(
        body, mesh=mesh, in_specs=placed, out_specs=(P(("tm", "space"), None), P()), check_vma=False
    )
```
